512 devices in a mesh: dap: 128 (over z, y_hi, x, core), head: 4 (over y_lo).
Axes of the slice: x: 4, y: 8 (y_hi: 2, y_lo: 4; y = y_hi * 4 + y_lo), z: 8, core: 2. Of those that a mesh axis runs over, the one named last changes fastest.
Arguments:
- alignment_activity: bfloat16 [128, 512, 256], P('dap'), may hold values from -6 to 6
- attend_standard_gain: float32 [256], replicated, may hold values from 0.25 to 1.75
- asking_projector: bfloat16 [256, 256], P(None, 'head'), may hold values from -0.5 to 0.5
- lookup_projector: bfloat16 [256, 256], P(None, 'head'), may hold values from -24 to 24
- content_projector: bfloat16 [256, 256], P(None, 'head'), may hold values from -0.375 to 0.375
- gating_projector: bfloat16 [256, 256], P(None, 'head'), may hold values from -0.75 to 0.75
- attend_result_projector: bfloat16 [256, 256], replicated, may hold values from -3 to 3
- tensor_standard_gain: float32 [256], replicated, may hold values from 0.25 to 1.75
- first_factor_projector: bfloat16 [256, 32], P(None, 'head'), may hold values from -0.375 to 0.375
- second_factor_projector: bfloat16 [256, 32], replicated, may hold values from -0.375 to 0.375
- flattened_to_grid_projector: bfloat16 [1024, 128], replicated, may hold values from -1.5 to 1.5
- grid_result_offset: float32 [128], replicated, may hold values from -3 to 3
Outputs:
- alignment_after_vertical: bfloat16 [128, 512, 256], P('dap')
- residue_grid_delta: bfloat16 [512, 512, 128], P(None, 'dap', 'head')
The draws below stay inside these ranges and needn't reach their ends.
All inputs are finite; a program needn't handle non-finite values.
Results may differ from the reference program's by a relative error of at most 0.018.
Values may be sent and summed in bfloat16 or wider, within the bound.
A program may use at most 64 MiB of HBM per device.

```python
import jax
import jax.numpy as jnp
from jax import lax

CM = 256
HEAD_COUNT = 8
HEAD_DIMENSION = 32
CC = 32
CZ = 128
SEQS = 128
NRES = 512
SLAB = 512


def shared_query(key):
    base = jax.random.normal(jax.random.fold_in(key, 11), (CM, HEAD_COUNT * HEAD_DIMENSION), jnp.float32)
    return jnp.clip(base, -4.0, 4.0) / CM ** 0.5


def draw_alignment_activity(key, part):
    key = jax.random.fold_in(key, 1)
    first = jax.random.fold_in(key, 0)
    return jnp.clip(jax.random.normal(first, (SEQS, NRES, CM), jnp.float32), -6.0, 6.0).astype(jnp.bfloat16)


def draw_asking_projector(key, part):
    base = shared_query(key)
    return base.astype(jnp.bfloat16)


def draw_lookup_projector(key, part):
    key = jax.random.fold_in(key, 3)
    fresh = jnp.clip(jax.random.normal(key, (CM, HEAD_COUNT * HEAD_DIMENSION), jnp.float32), -4.0, 4.0) / CM ** 0.5
    return fresh.astype(jnp.bfloat16)


def block_scale(key, shape, cuts, smallest, high):
    loudness = 1.0
    for dim, shards_of in cuts:
        draws = jax.random.uniform(jax.random.fold_in(jax.random.fold_in(key, 6), dim), (shards_of,), jnp.float32, smallest / len(cuts), high / len(cuts))
        loudness = loudness * jnp.repeat(jnp.exp(draws), shape[dim] // shards_of).reshape((-1,) + (1,) * (len(shape) - 1 - dim))
    return loudness


def scatter_about(key, extent, spread, limit, shards=(), held_as=jnp.bfloat16):
    factor_of = block_scale(key, extent, shards, -0.22, 0.18) if shards else 1.0
    array = jax.random.normal(key, extent, jnp.float32) * spread * factor_of
    return jnp.minimum(jnp.maximum(array, -limit), limit).astype(held_as)


def setup_inputs(seed: int = 0) -> dict:
    streams_of = jax.random.split(jax.random.key(seed), 13)
    return {
        "alignment_activity": draw_alignment_activity(jax.random.fold_in(streams_of[12], 71), 0),
        "attend_standard_gain": jnp.clip(1.0 + 0.15 * jax.random.normal(streams_of[1], (CM,), jnp.float32), 0.25, 1.75),
        "asking_projector": draw_asking_projector(jax.random.fold_in(streams_of[12], 71), 0),
        "lookup_projector": draw_lookup_projector(jax.random.fold_in(streams_of[12], 71), 0),
        "content_projector": scatter_about(streams_of[4], (CM, HEAD_COUNT * HEAD_DIMENSION), CM ** -0.5, 0.375, ((1, 4),)),
        "gating_projector": scatter_about(streams_of[5], (CM, HEAD_COUNT * HEAD_DIMENSION), (CM // 4) ** -0.5, 0.75, ((1, 4),)),
        "attend_result_projector": scatter_about(streams_of[6], (HEAD_COUNT * HEAD_DIMENSION, CM), (HEAD_COUNT * HEAD_DIMENSION // 64) ** -0.5, 3.0),
        "tensor_standard_gain": jnp.clip(1.0 + 0.15 * jax.random.normal(streams_of[7], (CM,), jnp.float32), 0.25, 1.75),
        "first_factor_projector": scatter_about(streams_of[8], (CM, CC), CM ** -0.5, 0.375, ((1, 4),)),
        "second_factor_projector": scatter_about(streams_of[9], (CM, CC), CM ** -0.5, 0.375),
        "flattened_to_grid_projector": scatter_about(streams_of[10], (CC * CC, CZ), (max(1, 2 * CC * CC // SEQS)) ** -0.5, 1.5),
        "grid_result_offset": scatter_about(streams_of[11], (CZ,), 0.5, 3.0, (), jnp.float32),
    }


EPS = 1e-05

def standardize_features(values_in, gain):
    values_in = values_in.astype(jnp.float32)
    mean = lax.optimization_barrier(jnp.mean(values_in, axis=-1, keepdims=True))
    centred = values_in - mean
    variance = lax.optimization_barrier(jnp.mean(centred * centred, axis=-1, keepdims=True))
    return centred * lax.rsqrt(variance + EPS) * gain.astype(jnp.float32)

def apply_projection_fn(standardized_sequences, asking_projector, lookup_projector, content_projector, gating_projector, attend_heads_list):
    leading_dims = standardized_sequences.shape[:-1]

    def apply_weight(coefficient_array):
        return jnp.dot(standardized_sequences, coefficient_array, preferred_element_type=jnp.float32).reshape(leading_dims + (attend_heads_list, HEAD_DIMENSION))
    query = apply_weight(asking_projector).astype(jnp.bfloat16)
    keys = apply_weight(lookup_projector).astype(jnp.bfloat16)
    values = apply_weight(content_projector).astype(jnp.bfloat16)
    gate = jax.nn.sigmoid(apply_weight(gating_projector)).astype(jnp.bfloat16)
    return jnp.concatenate([query, keys, values, gate], axis=-1)

def attend_column(block):
    block = block.astype(jnp.float32)
    query = block[..., :HEAD_DIMENSION]
    keys = block[..., HEAD_DIMENSION:2 * HEAD_DIMENSION]
    values = block[..., 2 * HEAD_DIMENSION:3 * HEAD_DIMENSION]
    gate = block[..., 3 * HEAD_DIMENSION:]
    scores = jnp.einsum('shd,thd->hst', query, keys) * HEAD_DIMENSION ** (-0.5)
    peak = lax.optimization_barrier(jnp.max(scores, axis=-1, keepdims=True))
    weights = jnp.exp(scores - peak)
    probs = (weights / lax.optimization_barrier(jnp.sum(weights, axis=-1, keepdims=True))).astype(jnp.bfloat16)
    mixed = jnp.einsum('hst,thd->shd', probs.astype(jnp.float32), values)
    return (mixed * gate).astype(jnp.bfloat16)

def reference(alignment_activity, attend_standard_gain, asking_projector, lookup_projector, content_projector, gating_projector, attend_result_projector, tensor_standard_gain, first_factor_projector, second_factor_projector, flattened_to_grid_projector, grid_result_offset):
    standardized_sequences = standardize_features(alignment_activity, attend_standard_gain).astype(jnp.bfloat16)
    stacked_tensor = apply_projection_fn(standardized_sequences, asking_projector, lookup_projector, content_projector, gating_projector, HEAD_COUNT)
    columns = jnp.moveaxis(stacked_tensor, 1, 0)
    mixed = jnp.moveaxis(lax.map(attend_column, columns), 0, 1)
    flat = mixed.reshape(SEQS, NRES, HEAD_COUNT * HEAD_DIMENSION)
    grid_increment = jnp.dot(flat, attend_result_projector, preferred_element_type=jnp.float32)
    alignment_after_vertical = (alignment_activity.astype(jnp.float32) + grid_increment).astype(jnp.bfloat16)
    second_standardized_sequences = standardize_features(alignment_after_vertical, tensor_standard_gain).astype(jnp.bfloat16)
    first_factor = jnp.dot(second_standardized_sequences, first_factor_projector, preferred_element_type=jnp.float32).astype(jnp.bfloat16)
    second_factor = jnp.dot(second_standardized_sequences, second_factor_projector, preferred_element_type=jnp.float32).astype(jnp.bfloat16)
    right_wide = second_factor.astype(jnp.float32)
    blocks = SLAB // 8
    left_slab = first_factor[:, :SLAB, :].reshape(SEQS, blocks, 8, CC)
    left_slab = jnp.moveaxis(left_slab, 1, 0)

    def slab_block(left_block):
        outer = jnp.einsum('sic,sje->ijce', left_block.astype(jnp.float32), right_wide) / SEQS
        outer = outer.astype(jnp.bfloat16).reshape(8, NRES, CC * CC)
        result = jnp.dot(outer, flattened_to_grid_projector, preferred_element_type=jnp.float32) + grid_result_offset.astype(jnp.float32)
        return result.astype(jnp.bfloat16)
    residue_grid_delta = lax.map(slab_block, left_slab).reshape(SLAB, NRES, CZ)
    return (alignment_after_vertical, residue_grid_delta)
```

```python
import functools

import jax
import jax.numpy as jnp
from jax import lax
from jax.experimental import pallas as pl
from jax.experimental.pallas import tpu as pltpu
from jax.sharding import PartitionSpec as P

MESH = pl.DeviceIdType.MESH
HEAD_DIMENSION = 32
XC = 8
EPS = 1e-05
BF = jnp.bfloat16
F32 = jnp.float32


def dot(a, b, ca, cb):
    return lax.dot_general(a, b, (((ca,), (cb,)), ((), ())), preferred_element_type=F32)


def standardize(v, gain):
    mean = jnp.mean(v, axis=-1, keepdims=True)
    centred = v - mean
    variance = jnp.mean(centred * centred, axis=-1, keepdims=True)
    return (centred * lax.rsqrt(variance + EPS) * gain).astype(BF)


def swap(src, tmp, dst):
    a, b, width = src.shape
    for i in range(width // 128):
        lanes = slice(i * 128, (i + 1) * 128)
        tmp[i] = src[:, :, lanes].astype(F32).reshape(a * b, 128)
        for k in range(b):
            dst[k, :, lanes] = tmp[i, pl.ds(k, a, stride=b), :].astype(BF)


def kernel(
    dims,
    x_ref, wq_ref, wk_ref, wv_ref, wg_ref, wo_ref, gain1_ref, gain2_ref, f1_ref, f2_ref, pw_ref, bias_ref,
    o0_ref, o1_ref,
    wsend, wall, s2t, r1, tmp, s2, r2, acol, lcol, rcol, l1, tmpl, left, right, z, res, ra1, tmpa, sa2,
    sem_s1, sem_r1, sem_sw, sem_rw, sem_s2, sem_r2, sem_sl1, sem_rl1, sem_sl2, sem_rl2, sem_sl3, sem_rl3,
    sem_sr, sem_rr, sem_sa1, sem_ra1, sem_sa2, sem_ra2, sem_sa3, sem_ra3, sem_sx, sem_rx, sem_loc,
):
    G, H, CM = dims
    X = XC // 2
    S = G * XC
    HW = wq_ref.shape[1]
    NH = HW // HEAD_DIMENSION
    FC = f1_ref.shape[1]
    CC = f2_ref.shape[1]
    CZ = pw_ref.shape[1]
    ZQ = CZ // H
    d = lax.axis_index("dap")
    h = lax.axis_index("head")
    g = d // XC
    xc = d % XC
    xx = xc // 2
    core = xc % 2

    def rcopy(src, dst, ssem, rsem, dd, hh):
        return pltpu.make_async_remote_copy(
            src_ref=src, dst_ref=dst, send_sem=ssem, recv_sem=rsem, device_id=(dd, hh), device_id_type=MESH
        )

    def each(n, f):
        def step(o, c):
            f(o)
            return c

        lax.fori_loop(1, n, step, 0)

    def dg(o):
        return ((g + o) % G) * XC + xc

    def dxc(o):
        return g * XC + (xc + o) % XC

    m = XC * h + xc
    xc_d = m // H
    slot = m % H
    own_writer = xc_d == xc

    barrier = pltpu.get_barrier_semaphore()

    def signal(dd, hh):
        pl.semaphore_signal(barrier, inc=1, device_id=(dd, hh), device_id_type=MESH)

    each(G, lambda o: signal(dg(o), h))
    each(XC, lambda o: signal(dxc(o), h))
    each(H, lambda o: signal(d, (h + o) % H))
    for k in range(H):
        ms = H * xc + k
        src_h, src_xc = ms // XC, ms % XC

        @pl.when(jnp.logical_not((src_h == h) & (src_xc == xc)))
        def _():
            signal(g * XC + src_xc, src_h)

    for i, w in enumerate((wq_ref, wk_ref, wv_ref, wg_ref)):
        wsend[i * HW : (i + 1) * HW, :] = w[...].astype(F32).T.astype(BF)
    f1t = jnp.concatenate([f1_ref[...].astype(F32), jnp.zeros((CM, 128 - FC), F32)], axis=1).T
    wsend[4 * HW :, :] = f1t[:16].astype(BF)
    s2t[...] = jnp.concatenate([f2_ref[...].astype(F32), jnp.zeros((CM, 128 - CC), F32)], axis=1).T[:CC].astype(BF)

    pl.semaphore_wait(barrier, (G - 1) + (XC - 1) + (H - 1) + H - jnp.where(own_writer, 1, 0))

    def a1(o):
        gg = (g + o) % G
        return rcopy(x_ref.at[gg, h], r1.at[g], sem_s1.at[gg], sem_r1.at[g], dg(o), h)

    each(G, lambda o: a1(o).start())
    loc1 = pltpu.make_async_copy(x_ref.at[g, h], r1.at[g], sem_loc.at[0])
    loc1.start()

    def aw(o):
        hh = (h + o) % H
        return rcopy(wsend, wall.at[h], sem_sw.at[hh], sem_rw.at[h], d, hh)

    each(H, lambda o: aw(o).start())
    loc2 = pltpu.make_async_copy(wsend, wall.at[h], sem_loc.at[1])
    loc2.start()

    def wait_r1(o):
        gg = (g + o) % G
        rcopy(x_ref.at[gg, h], r1.at[gg], sem_s1.at[gg], sem_r1.at[gg], dg(o), h).wait_recv()

    loc1.wait()
    each(G, wait_r1)

    swap(r1, tmp, s2)

    def a2(o):
        t = (xc + o) % XC
        rows = pl.ds(pl.multiple_of(xc * G, G), G)
        return rcopy(s2.at[t], r2.at[rows], sem_s2.at[t], sem_r2.at[xc], dxc(o), h)

    each(XC, lambda o: a2(o).start())
    r2[pl.ds(pl.multiple_of(xc * G, G), G), :] = s2[xc]

    def wait_r2(o):
        t = (xc + o) % XC
        rows = pl.ds(pl.multiple_of(t * G, G), G)
        rcopy(s2.at[t], r2.at[rows], sem_s2.at[t], sem_r2.at[t], dxc(o), h).wait_recv()

    each(XC, wait_r2)
    activity = r2[...].astype(F32)
    normed = standardize(activity, gain1_ref[...])

    def wait_w(o):
        hh = (h + o) % H
        rcopy(wsend, wall.at[hh], sem_sw.at[hh], sem_rw.at[hh], d, hh).wait_recv()

    loc2.wait()
    each(H, wait_w)

    mixed = []
    for hp in range(H):
        proj = dot(wall[hp, : 4 * HW, :], normed, 1, 1)
        query = proj[:HW].astype(BF)
        keys = proj[HW : 2 * HW].astype(BF)
        values = proj[2 * HW : 3 * HW].astype(BF)
        gate = jax.nn.sigmoid(proj[3 * HW :]).astype(BF).astype(F32)
        for e in range(NH):
            rows = slice(e * HEAD_DIMENSION, (e + 1) * HEAD_DIMENSION)
            scores = dot(keys[rows], query[rows], 0, 0) * HEAD_DIMENSION ** (-0.5)
            weights = jnp.exp(scores - jnp.max(scores, axis=0, keepdims=True))
            probs = (weights / jnp.sum(weights, axis=0, keepdims=True)).astype(BF)
            mixed.append((dot(values[rows], probs, 1, 0) * gate[rows]).astype(BF))
    mixed = jnp.concatenate(mixed, axis=0)
    after = (activity + dot(mixed, wo_ref[...], 0, 0)).astype(BF)
    acol[...] = after
    normed2 = standardize(after.astype(F32), gain2_ref[...])
    f1 = jnp.concatenate([wall[hp, 4 * HW :, :].astype(F32)[:FC] for hp in range(H)], axis=0).astype(BF)
    lcol[...] = dot(f1, normed2, 1, 1).astype(BF)
    rcol[...] = dot(s2t[...], normed2, 1, 1).astype(BF)

    def al1(o):
        gg = (g + o) % G
        return rcopy(lcol, l1.at[g], sem_sl1.at[gg], sem_rl1.at[g], dg(o), h)

    each(G, lambda o: al1(o).start())
    l1[g] = lcol[...]

    def ar(hh):
        return rcopy(rcol, right.at[slot], sem_sr.at[hh], sem_rr.at[slot], g * XC + xc_d, hh)

    for hh in range(H):
        here = own_writer & (h == hh)

        @pl.when(jnp.logical_not(here))
        def _():
            ar(hh).start()

        @pl.when(here)
        def _():
            right[slot] = rcol[...]

    def aa1(o):
        t = (xc + o) % XC
        rows = pl.ds(pl.multiple_of(t * G, G), G)
        return rcopy(acol.at[rows], ra1.at[xc], sem_sa1.at[t], sem_ra1.at[xc], dxc(o), h)

    each(XC, lambda o: aa1(o).start())
    ra1[xc] = acol[pl.ds(pl.multiple_of(xc * G, G), G), :]

    def wait_l1(o):
        gg = (g + o) % G
        rcopy(lcol, l1.at[gg], sem_sl1.at[gg], sem_rl1.at[gg], dg(o), h).wait_recv()

    each(G, wait_l1)
    tmpl[...] = l1[...].astype(F32).reshape(G * CC, S)
    own_rows = pl.ds(pl.multiple_of(core * X * G + xx * G, G), G)
    for c in range(CC):
        left[c, own_rows, :] = tmpl[pl.ds(c, G, stride=CC), :].astype(BF)

    def al2(o):
        t = (xx + o) % X
        dst = left.at[:, own_rows, :]
        return rcopy(dst, dst, sem_sl2.at[t], sem_rl2.at[xx], g * XC + 2 * t + core, h)

    each(X, lambda o: al2(o).start())

    def wait_a1(o):
        t = (xc + o) % XC
        rows = pl.ds(pl.multiple_of(t * G, G), G)
        rcopy(acol.at[rows], ra1.at[t], sem_sa1.at[t], sem_ra1.at[t], dxc(o), h).wait_recv()

    each(XC, wait_a1)
    swap(ra1, tmpa, sa2)

    def aa2(o):
        gg = (g + o) % G
        return rcopy(sa2.at[gg], o0_ref.at[g, h], sem_sa2.at[gg], sem_ra2.at[g], dg(o), h)

    each(G, lambda o: aa2(o).start())
    o0_ref[g, h] = sa2[g]

    for k in range(H):
        ms = H * xc + k
        src_h, src_xc = ms // XC, ms % XC

        @pl.when(jnp.logical_not((src_h == h) & (src_xc == xc)))
        def _():
            rcopy(rcol, right.at[k], sem_sr.at[0], sem_rr.at[k], g * XC + src_xc, src_h).wait_recv()

    for k in range(H):
        rk = right[k].astype(F32).T.astype(BF)
        for c in range(CC):
            z[c * S : (c + 1) * S, k * CZ : (k + 1) * CZ] = jnp.dot(
                rk, pw_ref[c * CC : (c + 1) * CC, :], preferred_element_type=F32
            ).astype(BF)

    def wait_l2(o):
        t = (xx + o) % X
        dst = left.at[:, pl.ds(pl.multiple_of(core * X * G + t * G, G), G), :]
        rcopy(dst, dst, sem_sl2.at[t], sem_rl2.at[t], g * XC + 2 * t + core, h).wait_recv()

    each(X, wait_l2)
    sib = g * XC + 2 * xx + (1 - core)
    mine = left.at[:, pl.ds(pl.multiple_of(core * X * G, X * G), X * G), :]
    theirs = left.at[:, pl.ds(pl.multiple_of((1 - core) * X * G, X * G), X * G), :]
    al3 = rcopy(mine, mine, sem_sl3, sem_rl3, sib, h)
    al3.start()

    def wait_a2(o):
        gg = (g + o) % G
        rcopy(sa2.at[gg], o0_ref.at[gg, h], sem_sa2.at[gg], sem_ra2.at[gg], dg(o), h).wait_recv()

    each(G, wait_a2)

    def aa3(o):
        hh = (h + o) % H
        return rcopy(o0_ref.at[:, h], o0_ref.at[:, h], sem_sa3.at[hh], sem_ra3.at[h], d, hh)

    each(H, lambda o: aa3(o).start())

    rcopy(theirs, theirs, sem_sl3, sem_rl3, sib, h).wait_recv()
    rows = jnp.concatenate([left[c] for c in range(CC)], axis=1)
    total = jnp.dot(rows, z[...], preferred_element_type=F32) * (1.0 / S)
    total = total + jnp.concatenate([bias_ref[...]] * H, axis=1)
    for hh in range(H):
        res[hh] = jnp.concatenate(
            [total[:, k * CZ + hh * ZQ : k * CZ + (hh + 1) * ZQ] for k in range(H)], axis=1
        ).astype(BF)

    def ax(o):
        hh = (h + o) % H
        return rcopy(res.at[hh], o1_ref.at[h], sem_sx.at[hh], sem_rx.at[h], d, hh)

    each(H, lambda o: ax(o).start())
    o1_ref[h] = res[h]

    def wait_x(o):
        hh = (h + o) % H
        rcopy(res.at[hh], o1_ref.at[hh], sem_sx.at[hh], sem_rx.at[hh], d, hh).wait_recv()

    each(H, wait_x)

    def wait_a3(o):
        hh = (h + o) % H
        rcopy(o0_ref.at[:, hh], o0_ref.at[:, hh], sem_sa3.at[hh], sem_ra3.at[hh], d, hh).wait_recv()

    each(H, wait_a3)
    each(G, lambda o: a1(o).wait_send())
    each(H, lambda o: aw(o).wait_send())
    each(XC, lambda o: a2(o).wait_send())
    each(G, lambda o: al1(o).wait_send())
    for hh in range(H):

        @pl.when(jnp.logical_not(own_writer & (h == hh)))
        def _():
            ar(hh).wait_send()

    each(XC, lambda o: aa1(o).wait_send())
    each(X, lambda o: al2(o).wait_send())
    each(G, lambda o: aa2(o).wait_send())
    al3.wait_send()
    each(H, lambda o: aa3(o).wait_send())
    each(H, lambda o: ax(o).wait_send())


def shards(mesh, x, gain1, wq, wk, wv, wg, wo, gain2, f1, f2, pw, bias):
    D, H = mesh.shape["dap"], mesh.shape["head"]
    G, X = D // XC, XC // 2
    S = D
    CM = x.shape[2]
    HW, FC, CC, CZ = wq.shape[1], f1.shape[1], f2.shape[1], pw.shape[1]
    vm = pl.BlockSpec(memory_space=pltpu.VMEM)
    dma = pltpu.SemaphoreType.DMA
    scratch = [
        pltpu.VMEM((4 * HW + 16, CM), BF),
        pltpu.VMEM((H, 4 * HW + 16, CM), BF),
        pltpu.VMEM((CC, CM), BF),
        pltpu.VMEM((G, XC, CM), BF),
        pltpu.VMEM((CM // 128, S, 128), F32),
        pltpu.VMEM((XC, G, CM), BF),
        pltpu.VMEM((S, CM), BF),
        pltpu.VMEM((S, CM), BF),
        pltpu.VMEM((CC, S), BF),
        pltpu.VMEM((CC, S), BF),
        pltpu.VMEM((G, CC, S), BF),
        pltpu.VMEM((G * CC, S), F32),
        pltpu.VMEM((CC, S, S), BF),
        pltpu.VMEM((H, CC, S), BF),
        pltpu.VMEM((CC * S, H * CZ), BF),
        pltpu.VMEM((H, S, CZ), BF),
        pltpu.VMEM((XC, G, CM), BF),
        pltpu.VMEM((CM // 128, S, 128), F32),
        pltpu.VMEM((G, XC, CM), BF),
    ]
    sems = [G, G, H, H, XC, XC, G, G, X, X, None, None, H, H, XC, XC, G, G, H, H, H, H, 2]
    scratch += [dma if n is None else dma((n,)) for n in sems]
    o0, o1 = pl.pallas_call(
        functools.partial(kernel, (G, H, CM)),
        out_shape=(
            jax.ShapeDtypeStruct((G, H, XC, CM), BF),
            jax.ShapeDtypeStruct((H, S, CZ), BF),
        ),
        in_specs=[pl.BlockSpec(memory_space=pl.ANY)] + [vm] * 11,
        out_specs=(vm, vm),
        scratch_shapes=scratch,
        compiler_params=pltpu.CompilerParams(
            collective_id=0, has_side_effects=True, vmem_limit_bytes=40 * 1024 * 1024
        ),
    )(
        x.reshape(G, H, XC, CM), wq, wk, wv, wg, wo, gain1.reshape(1, CM), gain2.reshape(1, CM), f1, f2, pw,
        bias.reshape(1, CZ),
    )
    after = o0.reshape(1, G * H * XC, CM)
    delta = o1.reshape(H, 2, X, G, H, CZ // H).transpose(3, 0, 2, 1, 4, 5)
    return after, delta.reshape(G * H * XC, H, CZ // H)


def solution(mesh):
    placed = (
        P("dap", None, None),
        P(),
        P(None, "head"),
        P(None, "head"),
        P(None, "head"),
        P(None, "head"),
        P(),
        P(),
        P(None, "head"),
        P(),
        P(),
        P(),
    )
    return jax.shard_map(
        functools.partial(shards, mesh),
        mesh=mesh,
        in_specs=placed,
        out_specs=(P("dap", None, None), P(None, "dap", "head")),
        check_vma=False,
    )
```

```python
import functools

import jax
import jax.numpy as jnp
from jax import lax
from jax.experimental import pallas as pl
from jax.experimental.pallas import tpu as pltpu
from jax.sharding import PartitionSpec as P

MESH = pl.DeviceIdType.MESH
HEAD_DIMENSION = 32
XC = 8
EPS = 1e-05
BF = jnp.bfloat16
F32 = jnp.float32


def dot(a, b, ca, cb):
    return lax.dot_general(a, b, (((ca,), (cb,)), ((), ())), preferred_element_type=F32)


def standardize(v, gain):
    mean = jnp.mean(v, axis=-1, keepdims=True)
    centred = v - mean
    variance = jnp.mean(centred * centred, axis=-1, keepdims=True)
    return (centred * lax.rsqrt(variance + EPS) * gain).astype(BF)


def swap(src, tmp, dst):
    a, b, width = src.shape
    for i in range(width // 128):
        lanes = slice(i * 128, (i + 1) * 128)
        tmp[i] = src[:, :, lanes].astype(F32).reshape(a * b, 128)
        for k in range(b):
            dst[k, :, lanes] = tmp[i, pl.ds(k, a, stride=b), :].astype(BF)


def kernel(
    dims,
    x_hbm, wq_hbm, wk_hbm, wv_hbm, wg_hbm, wo_hbm, gain1_hbm, gain2_hbm, f1_hbm, f2_hbm, pw_hbm, bias_hbm,
    o0_ref, o1_ref,
    wsend, wall, wo_ref, gain1_ref, gain2_ref, f1_ref, f2_ref, pw_ref, bias_ref, bias_t, place,
    r1, tmp, s2, r2, acol, lcol, rcol, l1, tmpl, left, right, z, res, rx, ra1, tmpa, sa2,
    sem_s1, sem_r1, sem_sw, sem_rw, sem_s2, sem_r2, sem_sl1, sem_rl1, sem_sl2, sem_rl2, sem_sl3, sem_rl3,
    sem_sr, sem_rr, sem_sa1, sem_ra1, sem_sa2, sem_ra2, sem_sa3, sem_ra3, sem_sx, sem_rx, sem_loc, sem_in,
):
    G, H, CM = dims
    X = XC // 2
    S = G * XC
    N = S * H
    HW = wq_hbm.shape[0]
    NH = HW // HEAD_DIMENSION
    FC = f1_hbm.shape[0]
    CC = f2_hbm.shape[0]
    CZ = pw_hbm.shape[1]
    ZQ = CZ // H
    d = lax.axis_index("dap")
    h = lax.axis_index("head")
    g = d // XC
    xc = d % XC
    xx = xc // 2
    core = xc % 2

    def rcopy(src, dst, ssem, rsem, dd, hh):
        return pltpu.make_async_remote_copy(
            src_ref=src, dst_ref=dst, send_sem=ssem, recv_sem=rsem, device_id=(dd, hh), device_id_type=MESH
        )

    def each(n, f):
        def step(o, c):
            f(o)
            return c

        lax.fori_loop(1, n, step, 0)

    def dg(o):
        return ((g + o) % G) * XC + xc

    def dxc(o):
        return g * XC + (xc + o) % XC

    m = XC * h + xc
    xc_d = m // H
    slot = m % H
    own_writer = xc_d == xc

    barrier = pltpu.get_barrier_semaphore()

    def signal(dd, hh):
        pl.semaphore_signal(barrier, inc=1, device_id=(dd, hh), device_id_type=MESH)

    each(G, lambda o: signal(dg(o), h))
    each(XC, lambda o: signal(dxc(o), h))
    each(H, lambda o: signal(d, (h + o) % H))
    for k in range(H):
        ms = H * xc + k
        src_h, src_xc = ms // XC, ms % XC

        @pl.when(jnp.logical_not((src_h == h) & (src_xc == xc)))
        def _():
            signal(g * XC + src_xc, src_h)

    ins = [
        pltpu.make_async_copy(w, wsend.at[pl.ds(i * HW, HW)], sem_in.at[i])
        for i, w in enumerate((wq_hbm, wk_hbm, wv_hbm, wg_hbm))
    ]
    for w, ref in (
        (f1_hbm, f1_ref), (f2_hbm, f2_ref), (gain1_hbm, gain1_ref), (gain2_hbm, gain2_ref), (wo_hbm, wo_ref),
        (bias_hbm, bias_ref), (pw_hbm, pw_ref),
    ):
        ins.append(pltpu.make_async_copy(w, ref, sem_in.at[len(ins)]))
    for copy in ins:
        copy.start()
    loc1 = pltpu.make_async_copy(x_hbm.at[g, h], r1.at[g], sem_loc.at[0])
    loc1.start()
    for copy in ins[:5]:
        copy.wait()
    wsend[4 * HW :, :] = jnp.concatenate(
        [f1_ref[...].astype(F32), jnp.zeros((16 - FC, CM), F32)], axis=0
    ).astype(BF) if FC < 16 else f1_ref[...]

    pl.semaphore_wait(barrier, (G - 1) + (XC - 1) + (H - 1) + H - jnp.where(own_writer, 1, 0))

    def a1(o):
        gg = (g + o) % G
        return rcopy(x_hbm.at[gg, h], r1.at[g], sem_s1.at[gg], sem_r1.at[g], dg(o), h)

    each(G, lambda o: a1(o).start())

    def aw(o):
        hh = (h + o) % H
        return rcopy(wsend, wall.at[h], sem_sw.at[hh], sem_rw.at[h], d, hh)

    each(H, lambda o: aw(o).start())
    loc2 = pltpu.make_async_copy(wsend, wall.at[h], sem_loc.at[1])
    loc2.start()

    for copy in ins[5:]:
        copy.wait()
    bias_t[...] = jnp.broadcast_to(bias_ref[...], (CZ, CZ)).T[:, :1] + jnp.zeros((CZ, S), F32)
    row = lax.broadcasted_iota(jnp.int32, (N, 1), 0)
    at = (row % G) * (H * XC) + (row // S) * XC + ((row // G) % X) * 2 + (row // (X * G)) % 2
    place[...] = jnp.where(lax.broadcasted_iota(jnp.int32, (N, N), 1) == at, 1.0, 0.0).astype(BF)

    def wait_r1(o):
        gg = (g + o) % G
        rcopy(x_hbm.at[gg, h], r1.at[gg], sem_s1.at[gg], sem_r1.at[gg], dg(o), h).wait_recv()

    loc1.wait()
    each(G, wait_r1)

    swap(r1, tmp, s2)

    def a2(o):
        t = (xc + o) % XC
        rows = pl.ds(pl.multiple_of(xc * G, G), G)
        return rcopy(s2.at[t], r2.at[rows], sem_s2.at[t], sem_r2.at[xc], dxc(o), h)

    each(XC, lambda o: a2(o).start())
    r2[pl.ds(pl.multiple_of(xc * G, G), G), :] = s2[xc]

    def wait_r2(o):
        t = (xc + o) % XC
        rows = pl.ds(pl.multiple_of(t * G, G), G)
        rcopy(s2.at[t], r2.at[rows], sem_s2.at[t], sem_r2.at[t], dxc(o), h).wait_recv()

    each(XC, wait_r2)
    activity = r2[...].astype(F32)
    normed = standardize(activity, gain1_ref[...])

    def wait_w(o):
        hh = (h + o) % H
        rcopy(wsend, wall.at[hh], sem_sw.at[hh], sem_rw.at[hh], d, hh).wait_recv()

    loc2.wait()
    each(H, wait_w)

    mixed = []
    for hp in range(H):
        proj = dot(wall[hp, : 4 * HW, :], normed, 1, 1)
        query = proj[:HW].astype(BF)
        keys = proj[HW : 2 * HW].astype(BF)
        values = proj[2 * HW : 3 * HW].astype(BF)
        gate = jax.nn.sigmoid(proj[3 * HW :]).astype(BF).astype(F32)
        for e in range(NH):
            rows = slice(e * HEAD_DIMENSION, (e + 1) * HEAD_DIMENSION)
            scores = dot(keys[rows], query[rows], 0, 0) * HEAD_DIMENSION ** (-0.5)
            weights = jnp.exp(scores - jnp.max(scores, axis=0, keepdims=True))
            probs = (weights / jnp.sum(weights, axis=0, keepdims=True)).astype(BF)
            mixed.append((dot(values[rows], probs, 1, 0) * gate[rows]).astype(BF))
    mixed = jnp.concatenate(mixed, axis=0)
    after = (activity + dot(mixed, wo_ref[...], 0, 0)).astype(BF)
    acol[...] = after
    normed2 = standardize(after.astype(F32), gain2_ref[...])
    f1 = jnp.concatenate([wall[hp, 4 * HW :, :].astype(F32)[:FC] for hp in range(H)], axis=0).astype(BF)
    lcol[...] = dot(f1, normed2, 1, 1).astype(BF)
    rcol[...] = dot(f2_ref[...], normed2, 1, 1).astype(BF)

    def al1(o):
        gg = (g + o) % G
        return rcopy(lcol, l1.at[g], sem_sl1.at[gg], sem_rl1.at[g], dg(o), h)

    each(G, lambda o: al1(o).start())
    l1[g] = lcol[...]

    def ar(hh):
        return rcopy(rcol, right.at[slot], sem_sr.at[hh], sem_rr.at[slot], g * XC + xc_d, hh)

    for hh in range(H):
        here = own_writer & (h == hh)

        @pl.when(jnp.logical_not(here))
        def _():
            ar(hh).start()

        @pl.when(here)
        def _():
            right[slot] = rcol[...]

    def aa1(o):
        t = (xc + o) % XC
        rows = pl.ds(pl.multiple_of(t * G, G), G)
        return rcopy(acol.at[rows], ra1.at[xc], sem_sa1.at[t], sem_ra1.at[xc], dxc(o), h)

    each(XC, lambda o: aa1(o).start())
    ra1[xc] = acol[pl.ds(pl.multiple_of(xc * G, G), G), :]

    def wait_l1(o):
        gg = (g + o) % G
        rcopy(lcol, l1.at[gg], sem_sl1.at[gg], sem_rl1.at[gg], dg(o), h).wait_recv()

    each(G, wait_l1)
    tmpl[...] = l1[...].astype(F32).reshape(G * CC, S)
    own_rows = pl.ds(pl.multiple_of(core * X * G + xx * G, G), G)
    for c in range(CC):
        left[c, own_rows, :] = tmpl[pl.ds(c, G, stride=CC), :].astype(BF)

    def al2(o):
        t = (xx + o) % X
        dst = left.at[:, own_rows, :]
        return rcopy(dst, dst, sem_sl2.at[t], sem_rl2.at[xx], g * XC + 2 * t + core, h)

    each(X, lambda o: al2(o).start())

    def wait_a1(o):
        t = (xc + o) % XC
        rows = pl.ds(pl.multiple_of(t * G, G), G)
        rcopy(acol.at[rows], ra1.at[t], sem_sa1.at[t], sem_ra1.at[t], dxc(o), h).wait_recv()

    each(XC, wait_a1)
    swap(ra1, tmpa, sa2)

    def aa2(o):
        gg = (g + o) % G
        return rcopy(sa2.at[gg], o0_ref.at[g, h], sem_sa2.at[gg], sem_ra2.at[g], dg(o), h)

    each(G, lambda o: aa2(o).start())
    o0_ref[g, h] = sa2[g]

    for k in range(H):
        ms = H * xc + k
        src_h, src_xc = ms // XC, ms % XC

        @pl.when(jnp.logical_not((src_h == h) & (src_xc == xc)))
        def _():
            rcopy(rcol, right.at[k], sem_sr.at[0], sem_rr.at[k], g * XC + src_xc, src_h).wait_recv()

    rights = jnp.concatenate([right[k] for k in range(H)], axis=1)
    for c in range(CC):
        zc = dot(pw_ref[c * CC : (c + 1) * CC, :], rights, 0, 0).astype(BF)
        for k in range(H):
            z[k * CZ : (k + 1) * CZ, c * S : (c + 1) * S] = zc[:, k * S : (k + 1) * S]

    def wait_l2(o):
        t = (xx + o) % X
        dst = left.at[:, pl.ds(pl.multiple_of(core * X * G + t * G, G), G), :]
        rcopy(dst, dst, sem_sl2.at[t], sem_rl2.at[t], g * XC + 2 * t + core, h).wait_recv()

    each(X, wait_l2)
    sib = g * XC + 2 * xx + (1 - core)
    mine = left.at[:, pl.ds(pl.multiple_of(core * X * G, X * G), X * G), :]
    theirs = left.at[:, pl.ds(pl.multiple_of((1 - core) * X * G, X * G), X * G), :]
    al3 = rcopy(mine, mine, sem_sl3, sem_rl3, sib, h)
    al3.start()

    def wait_a2(o):
        gg = (g + o) % G
        rcopy(sa2.at[gg], o0_ref.at[gg, h], sem_sa2.at[gg], sem_ra2.at[gg], dg(o), h).wait_recv()

    each(G, wait_a2)

    def aa3(o):
        hh = (h + o) % H
        return rcopy(o0_ref.at[:, h], o0_ref.at[:, h], sem_sa3.at[hh], sem_ra3.at[h], d, hh)

    each(H, lambda o: aa3(o).start())

    rcopy(theirs, theirs, sem_sl3, sem_rl3, sib, h).wait_recv()
    rows = jnp.concatenate([left[c] for c in range(CC)], axis=1)
    total = dot(z[...], rows, 1, 1) * (1.0 / S)
    for hh in range(H):
        for k in range(H):
            res[hh, k * ZQ : (k + 1) * ZQ, :] = (
                total[k * CZ + hh * ZQ : k * CZ + (hh + 1) * ZQ] + bias_t[hh * ZQ : (hh + 1) * ZQ]
            ).astype(BF)

    def ax(o):
        hh = (h + o) % H
        return rcopy(res.at[hh], rx.at[h], sem_sx.at[hh], sem_rx.at[h], d, hh)

    each(H, lambda o: ax(o).start())
    rx[h] = res[h]

    def wait_x(o):
        hh = (h + o) % H
        rcopy(res.at[hh], rx.at[hh], sem_sx.at[hh], sem_rx.at[hh], d, hh).wait_recv()

    each(H, wait_x)
    o1_ref[...] = jnp.dot(
        jnp.concatenate([rx[k] for k in range(H)], axis=1), place[...], preferred_element_type=F32
    ).astype(BF)

    def wait_a3(o):
        hh = (h + o) % H
        rcopy(o0_ref.at[:, hh], o0_ref.at[:, hh], sem_sa3.at[hh], sem_ra3.at[hh], d, hh).wait_recv()

    each(H, wait_a3)
    each(G, lambda o: a1(o).wait_send())
    each(H, lambda o: aw(o).wait_send())
    each(XC, lambda o: a2(o).wait_send())
    each(G, lambda o: al1(o).wait_send())
    for hh in range(H):

        @pl.when(jnp.logical_not(own_writer & (h == hh)))
        def _():
            ar(hh).wait_send()

    each(XC, lambda o: aa1(o).wait_send())
    each(X, lambda o: al2(o).wait_send())
    each(G, lambda o: aa2(o).wait_send())
    al3.wait_send()
    each(H, lambda o: aa3(o).wait_send())
    each(H, lambda o: ax(o).wait_send())


def shards(mesh, x, gain1, wq, wk, wv, wg, wo, gain2, f1, f2, pw, bias):
    D, H = mesh.shape["dap"], mesh.shape["head"]
    G, X = D // XC, XC // 2
    S = D
    CM = x.shape[2]
    HW, FC, CC, CZ = wq.shape[1], f1.shape[1], f2.shape[1], pw.shape[1]
    vm = pl.BlockSpec(memory_space=pltpu.VMEM)
    hbm = pl.BlockSpec(memory_space=pltpu.HBM)
    dma = pltpu.SemaphoreType.DMA
    scratch = [
        pltpu.VMEM((4 * HW + 16, CM), BF),
        pltpu.VMEM((H, 4 * HW + 16, CM), BF),
        pltpu.VMEM((CM, CM), BF),
        pltpu.VMEM((1, CM), F32),
        pltpu.VMEM((1, CM), F32),
        pltpu.VMEM((FC, CM), BF),
        pltpu.VMEM((CC, CM), BF),
        pltpu.VMEM((CC * CC, CZ), BF),
        pltpu.VMEM((1, CZ), F32),
        pltpu.VMEM((CZ, S), F32),
        pltpu.VMEM((S * H, S * H), BF),
        pltpu.VMEM((G, XC, CM), BF),
        pltpu.VMEM((CM // 128, S, 128), F32),
        pltpu.VMEM((XC, G, CM), BF),
        pltpu.VMEM((S, CM), BF),
        pltpu.VMEM((S, CM), BF),
        pltpu.VMEM((CC, S), BF),
        pltpu.VMEM((CC, S), BF),
        pltpu.VMEM((G, CC, S), BF),
        pltpu.VMEM((G * CC, S), F32),
        pltpu.VMEM((CC, S, S), BF),
        pltpu.VMEM((H, CC, S), BF),
        pltpu.VMEM((H * CZ, CC * S), BF),
        pltpu.VMEM((H, CZ, S), BF),
        pltpu.VMEM((H, CZ, S), BF),
        pltpu.VMEM((XC, G, CM), BF),
        pltpu.VMEM((CM // 128, S, 128), F32),
        pltpu.VMEM((G, XC, CM), BF),
    ]
    sems = [G, G, H, H, XC, XC, G, G, X, X, None, None, H, H, XC, XC, G, G, H, H, H, H, 2, 11]
    scratch += [dma if n is None else dma((n,)) for n in sems]
    o0, o1 = pl.pallas_call(
        functools.partial(kernel, (G, H, CM)),
        out_shape=(
            jax.ShapeDtypeStruct((G, H, XC, CM), BF),
            jax.ShapeDtypeStruct((CZ, H * S), BF),
        ),
        in_specs=[hbm] * 12,
        out_specs=(vm, vm),
        scratch_shapes=scratch,
        compiler_params=pltpu.CompilerParams(
            collective_id=0, has_side_effects=True, vmem_limit_bytes=40 * 1024 * 1024
        ),
    )(
        x.reshape(G, H, XC, CM), wq.T, wk.T, wv.T, wg.T, wo, gain1.reshape(1, CM), gain2.reshape(1, CM), f1.T, f2.T,
        pw, bias.reshape(1, CZ),
    )
    return o0.reshape(1, G * H * XC, CM), o1.reshape(H, CZ // H, H * S).transpose(2, 0, 1)


def solution(mesh):
    placed = (
        P("dap", None, None),
        P(),
        P(None, "head"),
        P(None, "head"),
        P(None, "head"),
        P(None, "head"),
        P(),
        P(),
        P(None, "head"),
        P(),
        P(),
        P(),
    )
    return jax.shard_map(
        functools.partial(shards, mesh),
        mesh=mesh,
        in_specs=placed,
        out_specs=(P("dap", None, None), P(None, "dap", "head")),
        check_vma=False,
    )
```

```python
import functools

import jax
import jax.numpy as jnp
from jax import lax
from jax.experimental import pallas as pl
from jax.experimental.pallas import tpu as pltpu
from jax.sharding import PartitionSpec as P

MESH = pl.DeviceIdType.MESH
HEAD_DIMENSION = 32
XC = 8
EPS = 1e-05
BF = jnp.bfloat16
F32 = jnp.float32


def dot(a, b, ca, cb):
    return lax.dot_general(a, b, (((ca,), (cb,)), ((), ())), preferred_element_type=F32)


def standardize(v, gain):
    mean = jnp.mean(v, axis=-1, keepdims=True)
    centred = v - mean
    variance = jnp.mean(centred * centred, axis=-1, keepdims=True)
    return (centred * lax.rsqrt(variance + EPS) * gain).astype(BF)


def rem(a, n):
    return lax.rem(a, jnp.int32(n))


def div(a, n):
    return lax.div(a, jnp.int32(n))


def swap(src, tmp, store, a, b):
    for i in range(src.shape[-1] // 128):
        lanes = slice(i * 128, (i + 1) * 128)
        tmp[i] = src[..., lanes].astype(F32).reshape(a * b, 128)
        for k in range(b):
            store(k, lanes, tmp[i, pl.ds(k, a, stride=b), :].astype(BF))


def turn(mats):
    n = len(mats)
    width = mats[0].shape[1]
    lane = lax.broadcasted_iota(jnp.int32, (1, width), 1)
    mats = list(mats)
    dist = n // 2
    while dist >= 1:
        lanes = dist * (width // n)
        low = (lane // lanes) % 2 == 0
        out = list(mats)
        for r in range(n):
            if (r // dist) % 2 == 0:
                a, b = mats[r], mats[r + dist]
                out[r] = jnp.where(low, a, pltpu.roll(b, lanes, 1))
                out[r + dist] = jnp.where(low, pltpu.roll(a, width - lanes, 1), b)
        mats = out
        dist //= 2
    return mats


def kernel(
    dims,
    x_hbm, wq_hbm, wk_hbm, wv_hbm, wg_hbm, wo_hbm, gain1_hbm, gain2_hbm, f1_hbm, f2_hbm, pw_hbm, bias_hbm,
    o0_ref, o1_ref,
    wall, wo_ref, gain1_ref, gain2_ref, f1_ref, f2_ref, pw_ref, bias_ref, place,
    r1, r1c, tmp, s2, s2c, r2, mixed, acol, lcol, rcol, l1, tmpl, left, right, res, rx, ra1, tmpa, sa2, ra2,
    sem_s1, sem_r1, sem_s1c, sem_r1c, sem_sw, sem_rw, sem_sv, sem_rv, sem_s2, sem_s2c, sem_r2, sem_sl1, sem_rl1,
    sem_sl3, sem_rl3, sem_sr, sem_rr, sem_sa1, sem_ra1, sem_sa2, sem_ra2, sem_sa3, sem_ra3, sem_sx, sem_rx,
    sem_loc, sem_in,
):
    Z, H, CM = dims
    X = XC // 2
    H2 = H // 2
    G = 2 * Z
    S = G * XC
    N = S * H
    HW = wq_hbm.shape[0]
    NH = HW // HEAD_DIMENSION
    FC = f1_hbm.shape[0]
    CC = f2_hbm.shape[0]
    CZ = pw_hbm.shape[1]
    WR = wall.shape[1] // 2
    d = lax.axis_index("dap")
    h = lax.axis_index("head")
    z = div(d, 2 * XC)
    yh = rem(div(d, XC), 2)
    xc = rem(d, XC)
    xx = div(xc, 2)
    core = rem(xc, 2)
    oy = 1 - yh
    block = (z * 2 + yh) * XC
    cross = (z * 2 + oy) * XC
    sib = block + 2 * xx + (1 - core)
    edge = (h == 0) | (h == H - 1)
    lo = jnp.where(h == 0, H2, 0)
    h_src = jnp.where(h < H2, H - 1, 0)

    def rcopy(src, dst, ssem, rsem, dd, hh):
        return pltpu.make_async_remote_copy(
            src_ref=src, dst_ref=dst, send_sem=ssem, recv_sem=rsem, device_id=(dd, hh), device_id_type=MESH
        )

    def each(n, f, first=1):
        def step(o, c):
            f(o)
            return c

        if n > first:
            lax.fori_loop(first, n, step, 0)

    def zz(o):
        return rem(z + o, Z)

    def dz(o):
        return (zz(o) * 2 + yh) * XC + xc

    def dm(o):
        return (zz(o) * 2 + oy) * XC + xc

    def tx(o):
        return rem(xc + o, XC)

    def th(o):
        return rem(h + o, H)

    barrier = pltpu.get_barrier_semaphore()

    def signal(dd, hh):
        pl.semaphore_signal(barrier, inc=1, device_id=(dd, hh), device_id_type=MESH)

    for o in range(1, XC):
        signal(block + tx(o), h)
    for o in range(1, Z):
        signal(dz(o), h)
    for o in range(Z):
        signal(dm(o), H - 1 - h)
    for o in range(XC):
        signal(cross + o, h_src)
    for o in range(H):
        signal(cross + xc, o)
    for k in range(1, H):
        hh = th(k)
        for o in range(XC):
            signal(block + o, hh)

    ins = [
        pltpu.make_async_copy(w, wall.at[h, pl.ds(i * HW, HW)], sem_in.at[i])
        for i, w in enumerate((wq_hbm, wk_hbm, wv_hbm, wg_hbm))
    ]
    for w, ref in (
        (f1_hbm, f1_ref), (f2_hbm, f2_ref), (gain1_hbm, gain1_ref), (gain2_hbm, gain2_ref), (wo_hbm, wo_ref),
        (bias_hbm, bias_ref), (pw_hbm, pw_ref),
    ):
        ins.append(pltpu.make_async_copy(w, ref, sem_in.at[len(ins)]))
    for copy in ins:
        copy.start()
    loc1 = pltpu.make_async_copy(x_hbm.at[z, yh, h], r1.at[z], sem_loc.at[0])
    loc1c = pltpu.make_async_copy(x_hbm.at[z, oy, pl.ds(lo, H2)], r1c.at[z], sem_loc.at[1])
    loc1.start()
    loc1c.start()

    pl.semaphore_wait(barrier, (Z - 1) + Z + (XC * H - 1) + H + jnp.where(edge, XC * H2, 0))

    def a1(o):
        t = zz(o)
        return rcopy(x_hbm.at[t, yh, h], r1.at[z], sem_s1.at[t], sem_r1.at[z], dz(o), h)

    def a1c(o):
        t = zz(o)
        return rcopy(x_hbm.at[t, oy, pl.ds(lo, H2)], r1c.at[z], sem_s1c.at[t], sem_r1c.at[z], dz(o), h)

    @pl.when(edge)
    def _():
        each(Z, lambda o: a1c(o).start())

    each(Z, lambda o: a1(o).start())

    for copy in ins[:5]:
        copy.wait()
    wall[h, 4 * HW :, :] = jnp.concatenate(
        [f1_ref[...].astype(F32), jnp.zeros((2 * WR - 4 * HW - FC, CM), F32)], axis=0
    ).astype(BF)
    half = pl.ds(pl.multiple_of(core * WR, 16), WR)
    other = pl.ds(pl.multiple_of((1 - core) * WR, 16), WR)

    def aw(o):
        hh = th(o)
        return rcopy(wall.at[h, half], wall.at[h, half], sem_sw.at[hh], sem_rw.at[h], d, hh)

    each(H, lambda o: aw(o).start())

    for copy in ins[5:]:
        copy.wait()

    def wait_r1(o):
        t = zz(o)
        rcopy(x_hbm.at[t, yh, h], r1.at[t], sem_s1.at[t], sem_r1.at[t], dz(o), h).wait_recv()

    def wait_r1c(o):
        t = zz(o)
        rcopy(x_hbm.at[t, oy, pl.ds(lo, H2)], r1c.at[t], sem_s1c.at[t], sem_r1c.at[t], dz(o), h).wait_recv()

    loc1.wait()
    loc1c.wait()

    def a2c(i, t):
        return rcopy(
            s2c.at[i, t], r2.at[yh, xc], sem_s2c.at[i * XC + t], sem_r2.at[yh * XC + xc], cross + t, lo + i
        )

    @pl.when(edge)
    def _():
        each(Z, wait_r1c)
        for i in range(H2):

            def store(k, lanes, v):
                s2c[i, k, :, lanes] = v

            swap(r1c.at[:, i], tmp, store, Z, XC)
            each(XC, lambda t: a2c(i, t).start(), 0)

    each(Z, wait_r1)

    def store_s2(k, lanes, v):
        s2[k, :, lanes] = v

    swap(r1, tmp, store_s2, Z, XC)

    def a2(o):
        t = tx(o)
        return rcopy(s2.at[t], r2.at[yh, xc], sem_s2.at[t], sem_r2.at[yh * XC + xc], block + t, h)

    each(XC, lambda o: a2(o).start())
    r2[yh, xc] = s2[xc]

    row = lax.broadcasted_iota(jnp.int32, (N, 1), 0)
    src = row // (2 * G)
    mirror = (row // Z) % 2
    src_h = jnp.where(mirror == 1, H - 1 - src % H, src % H)
    src_y = jnp.where(mirror == 1, oy, yh)
    at = ((row % Z) * 2 + src_y) * (H * XC) + src_h * XC + (src // H) * 2 + (row // G) % 2
    place[...] = jnp.where(lax.broadcasted_iota(jnp.int32, (N, N), 1) == at, 1.0, 0.0).astype(BF)

    def wait_r2(o):
        t = tx(o)
        rcopy(s2.at[t], r2.at[yh, t], sem_s2.at[t], sem_r2.at[yh * XC + t], block + t, h).wait_recv()

    def wait_r2c(t):
        rcopy(s2.at[t], r2.at[oy, t], sem_s2.at[t], sem_r2.at[oy * XC + t], cross + t, h_src).wait_recv()

    each(XC, wait_r2)
    each(XC, wait_r2c, 0)

    def av(o):
        hh = th(o)
        return rcopy(wall.at[hh, half], wall.at[hh, half], sem_sv.at[hh], sem_rv.at[hh], sib, h)

    def pass_w(o):
        hh = th(o)
        rcopy(wall.at[hh, half], wall.at[hh, half], sem_sw.at[hh], sem_rw.at[hh], d, hh).wait_recv()
        av(o).start()

    each(H, pass_w)
    activity = r2[...].astype(F32).reshape(S, CM)
    normed = standardize(activity, gain1_ref[...])

    for o in range(H):
        hh = th(o)
        if o > 0:
            rcopy(wall.at[hh, other], wall.at[hh, other], sem_sv.at[hh], sem_rv.at[hh], sib, h).wait_recv()
        proj = dot(wall[hh, : 4 * HW, :], normed, 1, 1)
        query = proj[:HW].astype(BF)
        keys = proj[HW : 2 * HW].astype(BF)
        values = proj[2 * HW : 3 * HW].astype(BF)
        gate = jax.nn.sigmoid(proj[3 * HW :]).astype(BF).astype(F32)
        parts = []
        for e in range(NH):
            rows = slice(e * HEAD_DIMENSION, (e + 1) * HEAD_DIMENSION)
            scores = dot(keys[rows], query[rows], 0, 0) * HEAD_DIMENSION ** (-0.5)
            weights = jnp.exp(scores - jnp.max(scores, axis=0, keepdims=True))
            probs = (weights / jnp.sum(weights, axis=0, keepdims=True)).astype(BF)
            parts.append((dot(values[rows], probs, 1, 0) * gate[rows]).astype(BF))
        mixed[pl.ds(pl.multiple_of(hh * HW, HW), HW), :] = jnp.concatenate(parts, axis=0)
    after = (activity + dot(mixed[...], wo_ref[...], 0, 0)).astype(BF).astype(F32)
    acol[...] = after.reshape(2, XC, Z, CM).astype(BF)
    normed2 = standardize(after, gain2_ref[...])
    f1 = jnp.concatenate([wall[k, 4 * HW :, :].astype(F32)[:FC] for k in range(H)], axis=0).astype(BF)
    lcol[...] = dot(f1, normed2, 1, 1).astype(BF)
    rcol[...] = dot(f2_ref[...], normed2, 1, 1).astype(BF)

    def al1(o):
        return rcopy(lcol, l1.at[z], sem_sl1.at[o], sem_rl1.at[z], dz(o), h)

    def al1m(o):
        return rcopy(lcol, l1.at[Z + z], sem_sl1.at[Z + o], sem_rl1.at[Z + z], dm(o), H - 1 - h)

    each(Z, lambda o: al1m(o).start(), 0)
    each(Z, lambda o: al1(o).start())
    l1[z] = lcol[...]

    core_d = div(xc, H)
    slot = h * H + rem(xc, H)

    def ar(o):
        x2 = rem(xx + div(o, H), X)
        return rcopy(rcol, right.at[slot], sem_sr.at[o], sem_rr.at[slot], block + 2 * x2 + core_d, th(rem(o, H)))

    @pl.when(core == core_d)
    def _():
        right[slot] = rcol[...]

    @pl.when(core != core_d)
    def _():
        ar(jnp.int32(0)).start()

    each(X * H, lambda o: ar(o).start())

    def aa1(o):
        t = tx(o)
        return rcopy(acol.at[:, t], ra1.at[xc], sem_sa1.at[t], sem_ra1.at[xc], block + t, h)

    each(XC, lambda o: aa1(o).start())
    ra1[xc] = acol[:, xc]

    def wait_a1(o):
        t = tx(o)
        rcopy(acol.at[:, t], ra1.at[t], sem_sa1.at[t], sem_ra1.at[t], block + t, h).wait_recv()

    each(XC, wait_a1)

    def store_a2(k, lanes, v):
        sa2[k // Z, k % Z, :, lanes] = v

    swap(ra1, tmpa, store_a2, XC, G)

    def aa2(o):
        t = zz(o)
        return rcopy(sa2.at[:, t], ra2.at[:, z], sem_sa2.at[t], sem_ra2.at[z], dz(o), h)

    each(Z, lambda o: aa2(o).start())
    ra2[:, z] = sa2[:, z]

    def wait_l1(k):
        rcopy(lcol, l1.at[k], sem_sl1.at[0], sem_rl1.at[k], d, h).wait_recv()

    each(Z, lambda o: wait_l1(zz(o)))
    each(Z, lambda o: wait_l1(Z + o), 0)
    tmpl[...] = l1[...].astype(F32).reshape(G * CC, S)
    for c in range(CC):
        left[0, c] = tmpl[pl.ds(c, G, stride=CC), :].astype(BF)
    al3 = rcopy(left.at[0], left.at[1], sem_sl3, sem_rl3, sib, h)
    al3.start()

    for k in range(X * H):
        from_h, from_xc = k // H, core * H + k % H

        @pl.when(jnp.logical_not((from_h == h) & (from_xc == xc)))
        def _():
            rcopy(rcol, right.at[k], sem_sr.at[0], sem_rr.at[k], block + from_xc, from_h).wait_recv()

    own = xx * H + h

    def ax(side, x2, hh):
        k = (side * X + x2) * H + hh
        at_core = core if side == 0 else 1 - core
        return rcopy(
            res.at[side, x2 * H + hh], rx.at[own, at_core], sem_sx.at[k], sem_rx.at[own * 2 + at_core],
            block + 2 * x2 + core, hh,
        )

    def pair_half(side):
        lefts = left[side].reshape(CC * G, S)
        flats = []
        for x2 in range(X):
            outer = dot(lefts, right[x2 * H : (x2 + 1) * H].reshape(H * CC, S), 1, 1) * (1.0 / S)
            flat = [[] for _ in range(H)]
            for c in range(0, CC, H):
                for k, part in enumerate(turn([outer[(c + r) * G : (c + r + 1) * G] for r in range(H)])):
                    flat[k].append(part.astype(BF))
            flats += [jnp.concatenate(f, axis=1) for f in flat]
        total = jnp.dot(jnp.concatenate(flats, axis=0), pw_ref[...], preferred_element_type=F32) + bias_ref[...]
        for x2 in range(X):
            base = x2 * H * G
            for hh, part in enumerate(turn([total[base + k * G : base + (k + 1) * G] for k in range(H)])):
                res[side, x2 * H + hh] = part.astype(BF)
                here = (x2 == xx) & (hh == h)

                @pl.when(here)
                def _():
                    rx[own, core if side == 0 else 1 - core] = res[side, x2 * H + hh]

                @pl.when(jnp.logical_not(here))
                def _():
                    ax(side, x2, hh).start()

    pair_half(0)

    def wait_a2(o):
        t = zz(o)
        rcopy(sa2.at[:, t], ra2.at[:, t], sem_sa2.at[t], sem_ra2.at[t], dz(o), h).wait_recv()

    each(Z, wait_a2)

    def aa3(o):
        return rcopy(
            ra2.at[yh], o0_ref.at[:, yh, h], sem_sa3.at[o], sem_ra3.at[yh * H + h], block + xc, th(o)
        )

    def aa3c(o):
        return rcopy(
            ra2.at[oy], o0_ref.at[:, yh, h], sem_sa3.at[H + o], sem_ra3.at[yh * H + h], cross + xc, o
        )

    each(H, lambda o: aa3c(o).start(), 0)
    each(H, lambda o: aa3(o).start())
    o0_ref[:, yh, h] = ra2[yh]

    rcopy(left.at[0], left.at[1], sem_sl3, sem_rl3, sib, h).wait_recv()
    pair_half(1)

    for x2 in range(X):
        for hh in range(H):
            k = x2 * H + hh

            @pl.when(k != own)
            def _():
                for c in range(2):
                    rcopy(
                        res.at[0, k], rx.at[k, c], sem_sx.at[k], sem_rx.at[k * 2 + c], block + 2 * x2 + core, hh
                    ).wait_recv()

    o1_ref[...] = dot(rx[...].reshape(N, CZ), place[...], 0, 0).astype(BF)

    def wait_a3(o):
        hh = th(o)
        rcopy(ra2.at[yh], o0_ref.at[:, yh, hh], sem_sa3.at[o], sem_ra3.at[yh * H + hh], d, hh).wait_recv()

    def wait_a3c(o):
        rcopy(ra2.at[oy], o0_ref.at[:, oy, o], sem_sa3.at[H + o], sem_ra3.at[oy * H + o], cross + xc, o).wait_recv()

    each(H, wait_a3)
    each(H, wait_a3c, 0)
    each(Z, lambda o: a1(o).wait_send())

    @pl.when(edge)
    def _():
        each(Z, lambda o: a1c(o).wait_send())
        for i in range(H2):
            each(XC, lambda t: a2c(i, t).wait_send(), 0)

    each(H, lambda o: aw(o).wait_send())
    each(H, lambda o: av(o).wait_send())
    each(XC, lambda o: a2(o).wait_send())
    each(Z, lambda o: al1m(o).wait_send(), 0)
    each(Z, lambda o: al1(o).wait_send())

    @pl.when(core != core_d)
    def _():
        ar(jnp.int32(0)).wait_send()

    each(X * H, lambda o: ar(o).wait_send())
    each(XC, lambda o: aa1(o).wait_send())
    each(Z, lambda o: aa2(o).wait_send())
    al3.wait_send()
    each(H, lambda o: aa3c(o).wait_send(), 0)
    each(H, lambda o: aa3(o).wait_send())
    for side in range(2):
        for x2 in range(X):
            for hh in range(H):

                @pl.when(x2 * H + hh != own)
                def _():
                    ax(side, x2, hh).wait_send()


def shards(mesh, x, gain1, wq, wk, wv, wg, wo, gain2, f1, f2, pw, bias):
    D, H = mesh.shape["dap"], mesh.shape["head"]
    G, X = D // XC, XC // 2
    Z = G // 2
    S = D
    CM = x.shape[2]
    HW, FC, CC, CZ = wq.shape[1], f1.shape[1], f2.shape[1], pw.shape[1]
    vm = pl.BlockSpec(memory_space=pltpu.VMEM)
    hbm = pl.BlockSpec(memory_space=pltpu.HBM)
    dma = pltpu.SemaphoreType.DMA
    scratch = [
        pltpu.VMEM((H, 4 * HW + 32, CM), BF),
        pltpu.VMEM((CM, CM), BF),
        pltpu.VMEM((1, CM), F32),
        pltpu.VMEM((1, CM), F32),
        pltpu.VMEM((FC, CM), BF),
        pltpu.VMEM((CC, CM), BF),
        pltpu.VMEM((CC * CC, CZ), BF),
        pltpu.VMEM((1, CZ), F32),
        pltpu.VMEM((S * H, S * H), BF),
        pltpu.VMEM((Z, XC, CM), BF),
        pltpu.VMEM((Z, H // 2, XC, CM), BF),
        pltpu.VMEM((CM // 128, Z * XC, 128), F32),
        pltpu.VMEM((XC, Z, CM), BF),
        pltpu.VMEM((H // 2, XC, Z, CM), BF),
        pltpu.VMEM((2, XC, Z, CM), BF),
        pltpu.VMEM((CM, S), BF),
        pltpu.VMEM((2, XC, Z, CM), BF),
        pltpu.VMEM((CC, S), BF),
        pltpu.VMEM((CC, S), BF),
        pltpu.VMEM((G, CC, S), BF),
        pltpu.VMEM((G * CC, S), F32),
        pltpu.VMEM((2, CC, G, S), BF),
        pltpu.VMEM((X * H, CC, S), BF),
        pltpu.VMEM((2, X * H, G, CZ), BF),
        pltpu.VMEM((X * H, 2, G, CZ), BF),
        pltpu.VMEM((XC, 2, Z, CM), BF),
        pltpu.VMEM((CM // 128, S, 128), F32),
        pltpu.VMEM((2, Z, XC, CM), BF),
        pltpu.VMEM((2, Z, XC, CM), BF),
    ]
    sems = [
        Z, Z, Z, Z, H, H, H, H, XC, H // 2 * XC, 2 * XC, G, G,
        None, None, X * H, X * H, XC, XC, Z, Z, 2 * H, 2 * H, 2 * X * H, 2 * X * H,
        2, 11,
    ]
    scratch += [dma if n is None else dma((n,)) for n in sems]
    o0, o1 = pl.pallas_call(
        functools.partial(kernel, (Z, H, CM)),
        out_shape=(
            pltpu.VMEM((Z, 2, H, XC, CM), BF),
            pltpu.VMEM((CZ, H * S), BF),
        ),
        in_specs=[hbm] * 12,
        out_specs=(vm, vm),
        scratch_shapes=scratch,
        compiler_params=pltpu.CompilerParams(
            collective_id=0, has_side_effects=True, vmem_limit_bytes=60 * 1024 * 1024
        ),
    )(
        x.reshape(Z, 2, H, XC, CM), wq.T, wk.T, wv.T, wg.T, wo, gain1.reshape(1, CM), gain2.reshape(1, CM), f1.T, f2.T,
        pw, bias.reshape(1, CZ),
    )
    return o0.reshape(1, H * S, CM), o1.reshape(H, CZ // H, H * S).transpose(2, 0, 1)


def solution(mesh):
    placed = (
        P("dap", None, None),
        P(),
        P(None, "head"),
        P(None, "head"),
        P(None, "head"),
        P(None, "head"),
        P(),
        P(),
        P(None, "head"),
        P(),
        P(),
        P(),
    )
    return jax.shard_map(
        functools.partial(shards, mesh),
        mesh=mesh,
        in_specs=placed,
        out_specs=(P("dap", None, None), P(None, "dap", "head")),
        check_vma=False,
    )
```

```python
import functools

import jax
import jax.numpy as jnp
from jax import lax
from jax.experimental import pallas as pl
from jax.experimental.pallas import tpu as pltpu
from jax.sharding import PartitionSpec as P

MESH = pl.DeviceIdType.MESH
HEAD_DIMENSION = 32
XC = 8
EPS = 1e-05
BF = jnp.bfloat16
F32 = jnp.float32


def dot(a, b, ca, cb):
    return lax.dot_general(a, b, (((ca,), (cb,)), ((), ())), preferred_element_type=F32)


def standardize(v, gain):
    mean = jnp.mean(v, axis=-1, keepdims=True)
    centred = v - mean
    variance = jnp.mean(centred * centred, axis=-1, keepdims=True)
    return (centred * lax.rsqrt(variance + EPS) * gain).astype(BF)


def rem(a, n):
    return lax.rem(a, jnp.int32(n))


def div(a, n):
    return lax.div(a, jnp.int32(n))


def swap(src, tmp, store, a, b):
    for i in range(src.shape[-1] // 128):
        lanes = slice(i * 128, (i + 1) * 128)
        tmp[i] = src[..., lanes].astype(F32).reshape(a * b, 128)
        for k in range(b):
            store(k, lanes, tmp[i, pl.ds(k, a, stride=b), :].astype(BF))


def turn(mats):
    n = len(mats)
    width = mats[0].shape[1]
    lane = lax.broadcasted_iota(jnp.int32, (1, width), 1)
    mats = list(mats)
    dist = n // 2
    while dist >= 1:
        lanes = dist * (width // n)
        low = (lane // lanes) % 2 == 0
        out = list(mats)
        for r in range(n):
            if (r // dist) % 2 == 0:
                a, b = mats[r], mats[r + dist]
                out[r] = jnp.where(low, a, pltpu.roll(b, lanes, 1))
                out[r + dist] = jnp.where(low, pltpu.roll(a, width - lanes, 1), b)
        mats = out
        dist //= 2
    return mats


def kernel(
    dims,
    x_hbm, wq_hbm, wk_hbm, wv_hbm, wg_hbm, wo_hbm, gain1_hbm, gain2_hbm, f1_hbm, f2_hbm, pw_hbm, bias_hbm,
    o0_ref, o1_ref,
    wall, wo_ref, gain1_ref, gain2_ref, f1_ref, f2_ref, pw_ref, bias_ref, place,
    xs, xsc, r1, r1c, tmp, s2, s2c, r2, mixed, acol, lcol, rcol, l1, tmpl, left, right, res, rx, ra1, tmpa, sa2, ra2,
    sem_s1, sem_r1, sem_s1c, sem_r1c, sem_sw, sem_rw, sem_sv, sem_rv, sem_s2, sem_s2c, sem_r2, sem_sl1, sem_rl1,
    sem_sl3, sem_rl3, sem_sr, sem_rr, sem_sa1, sem_ra1, sem_sa2, sem_ra2, sem_sa3, sem_ra3, sem_sx, sem_rx,
    sem_loc, sem_in, ready,
):
    Z, H, CM = dims
    X = XC // 2
    H2 = H // 2
    G = 2 * Z
    S = G * XC
    N = S * H
    HW = wq_hbm.shape[0]
    NH = HW // HEAD_DIMENSION
    FC = f1_hbm.shape[0]
    CC = f2_hbm.shape[0]
    CZ = pw_hbm.shape[1]
    WR = wall.shape[1] // 2
    d = lax.axis_index("dap")
    h = lax.axis_index("head")
    z = div(d, 2 * XC)
    yh = rem(div(d, XC), 2)
    xc = rem(d, XC)
    xx = div(xc, 2)
    core = rem(xc, 2)
    oy = 1 - yh
    block = (z * 2 + yh) * XC
    cross = (z * 2 + oy) * XC
    sib = block + 2 * xx + (1 - core)
    edge = (h == 0) | (h == H - 1)
    lo = jnp.where(h == 0, H2, 0)
    h_src = jnp.where(h < H2, H - 1, 0)

    def rcopy(src, dst, ssem, rsem, dd, hh):
        return pltpu.make_async_remote_copy(
            src_ref=src, dst_ref=dst, send_sem=ssem, recv_sem=rsem, device_id=(dd, hh), device_id_type=MESH
        )

    def each(n, f, first=1):
        def step(o, c):
            f(o)
            return c

        if n > first:
            lax.fori_loop(first, n, step, 0)

    def zz(o):
        return rem(z + o, Z)

    def dz(o):
        return (zz(o) * 2 + yh) * XC + xc

    def dm(o):
        return (zz(o) * 2 + oy) * XC + xc

    def tx(o):
        return rem(xc + o, XC)

    def th(o):
        return rem(h + o, H)

    barrier = pltpu.get_barrier_semaphore()

    def signal(dd, hh):
        pl.semaphore_signal(barrier, inc=1, device_id=(dd, hh), device_id_type=MESH)

    for o in sorted(range(1, Z), key=lambda o: -min(o, Z - o)):
        signal(dz(o), h)
    for o in range(1, XC):
        signal(block + tx(o), h)
    for o in range(XC):
        signal(cross + o, h_src)
    for o in range(H):
        signal(cross + xc, o)
    for k in range(1, H):
        hh = th(k)
        for o in range(XC):
            signal(block + o, hh)

    loc1 = pltpu.make_async_copy(x_hbm.at[:, yh, h], xs, sem_loc.at[0])
    loc1c = pltpu.make_async_copy(x_hbm.at[:, oy, pl.ds(lo, H2)], xsc, sem_loc.at[1])
    loc1.start()
    loc1c.start()
    ins = [
        pltpu.make_async_copy(w, wall.at[h, pl.ds(i * HW, HW)], sem_in.at[i])
        for i, w in enumerate((wq_hbm, wk_hbm, wv_hbm, wg_hbm))
    ]
    for w, ref in (
        (f1_hbm, f1_ref), (f2_hbm, f2_ref), (gain1_hbm, gain1_ref), (gain2_hbm, gain2_ref), (wo_hbm, wo_ref),
        (bias_hbm, bias_ref), (pw_hbm, pw_ref),
    ):
        ins.append(pltpu.make_async_copy(w, ref, sem_in.at[len(ins)]))
    for copy in ins:
        copy.start()

    pl.semaphore_wait(barrier, (Z - 1) + (XC * H - 1) + H + jnp.where(edge, XC * H2, 0))
    loc1.wait()
    loc1c.wait()

    def a1(o):
        t = zz(o)
        return rcopy(xs.at[t], r1.at[z], sem_s1.at[t], sem_r1.at[z], dz(o), h)

    def a1c(o):
        t = zz(o)
        return rcopy(xsc.at[t], r1c.at[z], sem_s1c.at[t], sem_r1c.at[z], dz(o), h)

    @pl.when(edge)
    def _():
        each(Z, lambda o: a1c(o).start())

    each(Z, lambda o: a1(o).start())
    pl.semaphore_signal(ready, inc=1, device_id=(cross + xc, H - 1 - h), device_id_type=MESH)
    r1[z] = xs[z]
    r1c[z] = xsc[z]

    for copy in ins[:5]:
        copy.wait()
    wall[h, 4 * HW :, :] = jnp.concatenate(
        [f1_ref[...].astype(F32), jnp.zeros((2 * WR - 4 * HW - FC, CM), F32)], axis=0
    ).astype(BF)
    half = pl.ds(pl.multiple_of(core * WR, 16), WR)
    other = pl.ds(pl.multiple_of((1 - core) * WR, 16), WR)

    def aw(o):
        hh = th(o)
        return rcopy(wall.at[h, half], wall.at[h, half], sem_sw.at[hh], sem_rw.at[h], d, hh)

    each(H, lambda o: aw(o).start())

    for copy in ins[5:]:
        copy.wait()

    def wait_r1(o):
        t = zz(o)
        rcopy(xs.at[t], r1.at[t], sem_s1.at[t], sem_r1.at[t], dz(o), h).wait_recv()

    def wait_r1c(o):
        t = zz(o)
        rcopy(xsc.at[t], r1c.at[t], sem_s1c.at[t], sem_r1c.at[t], dz(o), h).wait_recv()

    def a2c(i, t):
        return rcopy(
            s2c.at[i, t], r2.at[yh, xc], sem_s2c.at[i * XC + t], sem_r2.at[yh * XC + xc], cross + t, lo + i
        )

    @pl.when(edge)
    def _():
        each(Z, wait_r1c)
        for i in range(H2):

            def store(k, lanes, v):
                s2c[i, k, :, lanes] = v

            swap(r1c.at[:, i], tmp, store, Z, XC)
            each(XC, lambda t: a2c(i, t).start(), 0)

    each(Z, wait_r1)

    def store_s2(k, lanes, v):
        s2[k, :, lanes] = v

    swap(r1, tmp, store_s2, Z, XC)

    def a2(o):
        t = tx(o)
        return rcopy(s2.at[t], r2.at[yh, xc], sem_s2.at[t], sem_r2.at[yh * XC + xc], block + t, h)

    each(XC, lambda o: a2(o).start())
    r2[yh, xc] = s2[xc]

    row = lax.broadcasted_iota(jnp.int32, (N, 1), 0)
    src = row // (2 * G)
    mirror = (row // Z) % 2
    src_h = jnp.where(mirror == 1, H - 1 - src % H, src % H)
    src_y = jnp.where(mirror == 1, oy, yh)
    at = ((row % Z) * 2 + src_y) * (H * XC) + src_h * XC + (src // H) * 2 + (row // G) % 2
    place[...] = jnp.where(lax.broadcasted_iota(jnp.int32, (N, N), 1) == at, 1.0, 0.0).astype(BF)

    def wait_r2(o):
        t = tx(o)
        rcopy(s2.at[t], r2.at[yh, t], sem_s2.at[t], sem_r2.at[yh * XC + t], block + t, h).wait_recv()

    def wait_r2c(t):
        rcopy(s2.at[t], r2.at[oy, t], sem_s2.at[t], sem_r2.at[oy * XC + t], cross + t, h_src).wait_recv()

    each(XC, wait_r2)
    each(XC, wait_r2c, 0)

    def av(o):
        hh = th(o)
        return rcopy(wall.at[hh, half], wall.at[hh, half], sem_sv.at[hh], sem_rv.at[hh], sib, h)

    def pass_w(o):
        hh = th(o)
        rcopy(wall.at[hh, half], wall.at[hh, half], sem_sw.at[hh], sem_rw.at[hh], d, hh).wait_recv()
        av(o).start()

    each(H, pass_w)
    activity = r2[...].astype(F32).reshape(S, CM)
    normed = standardize(activity, gain1_ref[...])

    for o in range(H):
        hh = th(o)
        if o > 0:
            rcopy(wall.at[hh, other], wall.at[hh, other], sem_sv.at[hh], sem_rv.at[hh], sib, h).wait_recv()
        proj = dot(wall[hh, : 4 * HW, :], normed, 1, 1)
        query = proj[:HW].astype(BF)
        keys = proj[HW : 2 * HW].astype(BF)
        values = proj[2 * HW : 3 * HW].astype(BF)
        gate = jax.nn.sigmoid(proj[3 * HW :]).astype(BF).astype(F32)
        parts = []
        for e in range(NH):
            rows = slice(e * HEAD_DIMENSION, (e + 1) * HEAD_DIMENSION)
            scores = dot(keys[rows], query[rows], 0, 0) * HEAD_DIMENSION ** (-0.5)
            weights = jnp.exp(scores - jnp.max(scores, axis=0, keepdims=True))
            probs = (weights / jnp.sum(weights, axis=0, keepdims=True)).astype(BF)
            parts.append((dot(values[rows], probs, 1, 0) * gate[rows]).astype(BF))
        mixed[pl.ds(pl.multiple_of(hh * HW, HW), HW), :] = jnp.concatenate(parts, axis=0)
    after = (activity + dot(mixed[...], wo_ref[...], 0, 0)).astype(BF).astype(F32)
    acol[...] = after.reshape(2, XC, Z, CM).astype(BF)
    def aa1(o):
        t = tx(o)
        return rcopy(acol.at[:, t], ra1.at[xc], sem_sa1.at[t], sem_ra1.at[xc], block + t, h)

    each(XC, lambda o: aa1(o).start())
    ra1[xc] = acol[:, xc]

    normed2 = standardize(after, gain2_ref[...])
    f1 = jnp.concatenate([wall[k, 4 * HW :, :].astype(F32)[:FC] for k in range(H)], axis=0).astype(BF)
    lcol[...] = dot(f1, normed2, 1, 1).astype(BF)
    rcol[...] = dot(f2_ref[...], normed2, 1, 1).astype(BF)

    def al1(o):
        return rcopy(lcol, l1.at[z], sem_sl1.at[o], sem_rl1.at[z], dz(o), h)

    def al1m(o):
        return rcopy(lcol, l1.at[Z + z], sem_sl1.at[Z + o], sem_rl1.at[Z + z], dm(o), H - 1 - h)

    pl.semaphore_wait(ready, 1)
    each(Z, lambda o: al1m(o).start(), 0)
    each(Z, lambda o: al1(o).start())
    l1[z] = lcol[...]

    core_d = div(xc, H)
    slot = h * H + rem(xc, H)

    def ar(o):
        x2 = rem(xx + div(o, H), X)
        return rcopy(rcol, right.at[slot], sem_sr.at[o], sem_rr.at[slot], block + 2 * x2 + core_d, th(rem(o, H)))

    @pl.when(core == core_d)
    def _():
        right[slot] = rcol[...]

    @pl.when(core != core_d)
    def _():
        ar(jnp.int32(0)).start()

    each(X * H, lambda o: ar(o).start())

    def wait_a1(o):
        t = tx(o)
        rcopy(acol.at[:, t], ra1.at[t], sem_sa1.at[t], sem_ra1.at[t], block + t, h).wait_recv()

    each(XC, wait_a1)

    def store_a2(k, lanes, v):
        sa2[k // Z, k % Z, :, lanes] = v

    swap(ra1, tmpa, store_a2, XC, G)

    def aa2(o):
        t = zz(o)
        return rcopy(sa2.at[:, t], ra2.at[:, z], sem_sa2.at[t], sem_ra2.at[z], dz(o), h)

    each(Z, lambda o: aa2(o).start())
    ra2[:, z] = sa2[:, z]

    def aa3(t, o):
        return rcopy(
            ra2.at[yh, t], o0_ref.at[t, yh, h], sem_sa3.at[o], sem_ra3.at[yh * H + h], block + xc, th(o)
        )

    def aa3c(t, o):
        return rcopy(
            ra2.at[oy, t], o0_ref.at[t, yh, h], sem_sa3.at[H + o], sem_ra3.at[yh * H + h], cross + xc, o
        )

    def ring(t):
        each(H, lambda o: aa3c(t, o).start(), 0)
        each(H, lambda o: aa3(t, o).start())

    def wait_a2(o):
        t = zz(o)
        rcopy(sa2.at[:, t], ra2.at[:, t], sem_sa2.at[t], sem_ra2.at[t], dz(o), h).wait_recv()
        ring(t)

    near = sorted(range(1, Z), key=lambda o: min(o, Z - o))
    ring(z)

    def wait_l1(k):
        rcopy(lcol, l1.at[k], sem_sl1.at[0], sem_rl1.at[k], d, h).wait_recv()

    each(Z, lambda o: wait_l1(zz(o)))
    each(Z, lambda o: wait_l1(Z + o), 0)
    tmpl[...] = l1[...].astype(F32).reshape(G * CC, S)
    for c in range(CC):
        left[0, c] = tmpl[pl.ds(c, G, stride=CC), :].astype(BF)
    al3 = rcopy(left.at[0], left.at[1], sem_sl3, sem_rl3, sib, h)
    al3.start()

    for k in range(X * H):
        from_h, from_xc = k // H, core * H + k % H

        @pl.when(jnp.logical_not((from_h == h) & (from_xc == xc)))
        def _():
            rcopy(rcol, right.at[k], sem_sr.at[0], sem_rr.at[k], block + from_xc, from_h).wait_recv()

    own = xx * H + h

    def ax(side, x2, hh):
        k = (side * X + x2) * H + hh
        at_core = core if side == 0 else 1 - core
        return rcopy(
            res.at[side, x2 * H + hh], rx.at[own, at_core], sem_sx.at[k], sem_rx.at[own * 2 + at_core],
            block + 2 * x2 + core, hh,
        )

    def pair_half(side):
        lefts = left[side].reshape(CC * G, S)
        flats = []
        for x2 in range(X):
            outer = dot(lefts, right[x2 * H : (x2 + 1) * H].reshape(H * CC, S), 1, 1) * (1.0 / S)
            flat = [[] for _ in range(H)]
            for c in range(0, CC, H):
                for k, part in enumerate(turn([outer[(c + r) * G : (c + r + 1) * G] for r in range(H)])):
                    flat[k].append(part.astype(BF))
            flats += [jnp.concatenate(f, axis=1) for f in flat]
        total = jnp.dot(jnp.concatenate(flats, axis=0), pw_ref[...], preferred_element_type=F32) + bias_ref[...]
        for x2 in range(X):
            base = x2 * H * G
            for hh, part in enumerate(turn([total[base + k * G : base + (k + 1) * G] for k in range(H)])):
                res[side, x2 * H + hh] = part.astype(BF)
                here = (x2 == xx) & (hh == h)

                @pl.when(here)
                def _():
                    rx[own, core if side == 0 else 1 - core] = res[side, x2 * H + hh]

                @pl.when(jnp.logical_not(here))
                def _():
                    ax(side, x2, hh).start()

    for o in near[:4]:
        wait_a2(o)
    pair_half(0)
    for o in near[4:]:
        wait_a2(o)
    o0_ref[:, yh, h] = ra2[yh]

    rcopy(left.at[0], left.at[1], sem_sl3, sem_rl3, sib, h).wait_recv()
    pair_half(1)

    for x2 in range(X):
        for hh in range(H):
            k = x2 * H + hh

            @pl.when(k != own)
            def _():
                for c in range(2):
                    rcopy(
                        res.at[0, k], rx.at[k, c], sem_sx.at[k], sem_rx.at[k * 2 + c], block + 2 * x2 + core, hh
                    ).wait_recv()

    o1_ref[...] = dot(rx[...].reshape(N, CZ), place[...], 0, 0).astype(BF)

    def wait_a3(o):
        hh = th(o)
        rcopy(ra2.at[yh], o0_ref.at[:, yh, hh], sem_sa3.at[o], sem_ra3.at[yh * H + hh], d, hh).wait()

    def wait_a3c(o):
        rcopy(ra2.at[oy], o0_ref.at[:, oy, o], sem_sa3.at[H + o], sem_ra3.at[oy * H + o], cross + xc, o).wait()

    each(H, wait_a3)
    each(H, wait_a3c, 0)
    each(Z, lambda o: a1(o).wait_send())

    @pl.when(edge)
    def _():
        each(Z, lambda o: a1c(o).wait_send())
        for i in range(H2):
            each(XC, lambda t: a2c(i, t).wait_send(), 0)

    each(H, lambda o: aw(o).wait_send())
    each(H, lambda o: av(o).wait_send())
    each(XC, lambda o: a2(o).wait_send())
    each(Z, lambda o: al1m(o).wait_send(), 0)
    each(Z, lambda o: al1(o).wait_send())

    @pl.when(core != core_d)
    def _():
        ar(jnp.int32(0)).wait_send()

    each(X * H, lambda o: ar(o).wait_send())
    each(XC, lambda o: aa1(o).wait_send())
    each(Z, lambda o: aa2(o).wait_send())
    al3.wait_send()
    for side in range(2):
        for x2 in range(X):
            for hh in range(H):

                @pl.when(x2 * H + hh != own)
                def _():
                    ax(side, x2, hh).wait_send()


def shards(mesh, x, gain1, wq, wk, wv, wg, wo, gain2, f1, f2, pw, bias):
    D, H = mesh.shape["dap"], mesh.shape["head"]
    G, X = D // XC, XC // 2
    Z = G // 2
    S = D
    CM = x.shape[2]
    HW, FC, CC, CZ = wq.shape[1], f1.shape[1], f2.shape[1], pw.shape[1]
    vm = pl.BlockSpec(memory_space=pltpu.VMEM)
    hbm = pl.BlockSpec(memory_space=pltpu.HBM)
    dma = pltpu.SemaphoreType.DMA
    scratch = [
        pltpu.VMEM((H, 4 * HW + 32, CM), BF),
        pltpu.VMEM((CM, CM), BF),
        pltpu.VMEM((1, CM), F32),
        pltpu.VMEM((1, CM), F32),
        pltpu.VMEM((FC, CM), BF),
        pltpu.VMEM((CC, CM), BF),
        pltpu.VMEM((CC * CC, CZ), BF),
        pltpu.VMEM((1, CZ), F32),
        pltpu.VMEM((S * H, S * H), BF),
        pltpu.VMEM((Z, XC, CM), BF),
        pltpu.VMEM((Z, H // 2, XC, CM), BF),
        pltpu.VMEM((Z, XC, CM), BF),
        pltpu.VMEM((Z, H // 2, XC, CM), BF),
        pltpu.VMEM((CM // 128, Z * XC, 128), F32),
        pltpu.VMEM((XC, Z, CM), BF),
        pltpu.VMEM((H // 2, XC, Z, CM), BF),
        pltpu.VMEM((2, XC, Z, CM), BF),
        pltpu.VMEM((CM, S), BF),
        pltpu.VMEM((2, XC, Z, CM), BF),
        pltpu.VMEM((CC, S), BF),
        pltpu.VMEM((CC, S), BF),
        pltpu.VMEM((G, CC, S), BF),
        pltpu.VMEM((G * CC, S), F32),
        pltpu.VMEM((2, CC, G, S), BF),
        pltpu.VMEM((X * H, CC, S), BF),
        pltpu.VMEM((2, X * H, G, CZ), BF),
        pltpu.VMEM((X * H, 2, G, CZ), BF),
        pltpu.VMEM((XC, 2, Z, CM), BF),
        pltpu.VMEM((CM // 128, S, 128), F32),
        pltpu.VMEM((2, Z, XC, CM), BF),
        pltpu.VMEM((2, Z, XC, CM), BF),
    ]
    sems = [
        Z, Z, Z, Z, H, H, H, H, XC, H // 2 * XC, 2 * XC, G, G,
        None, None, X * H, X * H, XC, XC, Z, Z, 2 * H, 2 * H, 2 * X * H, 2 * X * H,
        2, 11,
    ]
    scratch += [dma if n is None else dma((n,)) for n in sems]
    scratch.append(pltpu.SemaphoreType.REGULAR)
    o0, o1 = pl.pallas_call(
        functools.partial(kernel, (Z, H, CM)),
        out_shape=(
            pltpu.VMEM((Z, 2, H, XC, CM), BF),
            pltpu.VMEM((CZ, H * S), BF),
        ),
        in_specs=[hbm] * 12,
        out_specs=(vm, vm),
        scratch_shapes=scratch,
        compiler_params=pltpu.CompilerParams(
            collective_id=0, has_side_effects=True, vmem_limit_bytes=60 * 1024 * 1024
        ),
    )(
        x.reshape(Z, 2, H, XC, CM), wq.T, wk.T, wv.T, wg.T, wo, gain1.reshape(1, CM), gain2.reshape(1, CM), f1.T, f2.T,
        pw, bias.reshape(1, CZ),
    )
    return o0.reshape(1, H * S, CM), o1.reshape(H, CZ // H, H * S).transpose(2, 0, 1)


def solution(mesh):
    placed = (
        P("dap", None, None),
        P(),
        P(None, "head"),
        P(None, "head"),
        P(None, "head"),
        P(None, "head"),
        P(),
        P(),
        P(None, "head"),
        P(),
        P(),
        P(),
    )
    return jax.shard_map(
        functools.partial(shards, mesh),
        mesh=mesh,
        in_specs=placed,
        out_specs=(P("dap", None, None), P(None, "dap", "head")),
        check_vma=False,
    )
```

```python
import functools

import jax
import jax.numpy as jnp
from jax import lax
from jax.experimental import pallas as pl
from jax.experimental.pallas import tpu as pltpu
from jax.sharding import PartitionSpec as P

MESH = pl.DeviceIdType.MESH
HEAD_DIMENSION = 32
XC = 8
EPS = 1e-05
BF = jnp.bfloat16
F32 = jnp.float32


def dot(a, b, ca, cb):
    return lax.dot_general(a, b, (((ca,), (cb,)), ((), ())), preferred_element_type=F32)


def standardize(v, gain):
    mean = jnp.mean(v, axis=-1, keepdims=True)
    centred = v - mean
    variance = jnp.mean(centred * centred, axis=-1, keepdims=True)
    return (centred * lax.rsqrt(variance + EPS) * gain).astype(BF)


def rem(a, n):
    return lax.rem(a, jnp.int32(n))


def div(a, n):
    return lax.div(a, jnp.int32(n))


def swap(src, tmp, store, a, b):
    for i in range(src.shape[-1] // 128):
        lanes = slice(i * 128, (i + 1) * 128)
        tmp[i] = src[..., lanes].astype(F32).reshape(a * b, 128)
        for k in range(b):
            store(k, lanes, tmp[i, pl.ds(k, a, stride=b), :].astype(BF))


def turn(mats):
    n = len(mats)
    width = mats[0].shape[1]
    lane = lax.broadcasted_iota(jnp.int32, (1, width), 1)
    mats = list(mats)
    dist = n // 2
    while dist >= 1:
        lanes = dist * (width // n)
        low = (lane // lanes) % 2 == 0
        out = list(mats)
        for r in range(n):
            if (r // dist) % 2 == 0:
                a, b = mats[r], mats[r + dist]
                out[r] = jnp.where(low, a, pltpu.roll(b, lanes, 1))
                out[r + dist] = jnp.where(low, pltpu.roll(a, width - lanes, 1), b)
        mats = out
        dist //= 2
    return mats


def kernel(
    dims,
    x_hbm, wq_hbm, wk_hbm, wv_hbm, wg_hbm, wo_hbm, gain1_hbm, gain2_hbm, f1_hbm, f2_hbm, pw_hbm, bias_hbm,
    o0_ref, o1_ref,
    wall, wo_ref, gain1_ref, gain2_ref, f1_ref, f2_ref, pw_ref, bias_ref, place,
    xs, xsc, r1, r1c, tmp, s2, s2c, r2, mixed, acol, lcol, rcol, l1, tmpl, left, rights, right, res, rx, ra1, tmpa, sa2, ra2,
    sem_s1, sem_r1, sem_s1c, sem_r1c, sem_sw, sem_rw, sem_sv, sem_rv, sem_s2, sem_s2c, sem_r2, sem_sl1, sem_rl1,
    sem_sl3, sem_rl3, sem_sr, sem_rr, sem_sq, sem_rq, sem_sa1, sem_ra1, sem_sa2, sem_ra2, sem_sa3, sem_ra3, sem_sx, sem_rx,
    sem_loc, sem_in, ready,
):
    Z, H, CM = dims
    X = XC // 2
    H2 = H // 2
    G = 2 * Z
    S = G * XC
    N = S * H
    HW = wq_hbm.shape[0]
    NH = HW // HEAD_DIMENSION
    FC = f1_hbm.shape[0]
    CC = f2_hbm.shape[0]
    CZ = pw_hbm.shape[1]
    WR = wall.shape[1] // 2
    d = lax.axis_index("dap")
    h = lax.axis_index("head")
    z = div(d, 2 * XC)
    yh = rem(div(d, XC), 2)
    xc = rem(d, XC)
    xx = div(xc, 2)
    core = rem(xc, 2)
    oy = 1 - yh
    block = (z * 2 + yh) * XC
    cross = (z * 2 + oy) * XC
    sib = block + 2 * xx + (1 - core)
    edge = (h == 0) | (h == H - 1)
    lo = jnp.where(h == 0, H2, 0)
    h_src = jnp.where(h < H2, H - 1, 0)

    def rcopy(src, dst, ssem, rsem, dd, hh):
        return pltpu.make_async_remote_copy(
            src_ref=src, dst_ref=dst, send_sem=ssem, recv_sem=rsem, device_id=(dd, hh), device_id_type=MESH
        )

    def each(n, f, first=1):
        def step(o, c):
            f(o)
            return c

        if n > first:
            lax.fori_loop(first, n, step, 0)

    def every(n, f, first=1):
        for o in range(first, n):
            f(o)

    def zz(o):
        return rem(z + o, Z)

    def dz(o):
        return (zz(o) * 2 + yh) * XC + xc

    def dm(o):
        return (zz(o) * 2 + oy) * XC + xc

    def tx(o):
        return rem(xc + o, XC)

    def th(o):
        return rem(h + o, H)

    peers = [h, h + 1 - 2 * rem(h, 2), rem(h + 2, 4), 3 - h] if H == 4 else [th(o) for o in range(H)]

    barrier = pltpu.get_barrier_semaphore()

    def signal(dd, hh):
        pl.semaphore_signal(barrier, inc=1, device_id=(dd, hh), device_id_type=MESH)

    for o in sorted(range(1, Z), key=lambda o: -min(o, Z - o)):
        signal(dz(o), h)
    loc1 = pltpu.make_async_copy(x_hbm.at[:, yh, h], xs, sem_loc.at[0])
    loc1c = pltpu.make_async_copy(x_hbm.at[:, oy, pl.ds(lo, H2)], xsc, sem_loc.at[1])
    loc1.start()
    loc1c.start()
    for o in range(1, XC):
        signal(block + tx(o), h)
    for o in range(XC):
        signal(cross + o, h_src)
    for o in range(H):
        signal(cross + xc, o)
    for k in range(1, H):
        hh = th(k)
        for o in range(XC):
            signal(block + o, hh)

    ins = [
        pltpu.make_async_copy(w, wall.at[h, pl.ds(i * HW, HW)], sem_in.at[i])
        for i, w in enumerate((wq_hbm, wk_hbm, wv_hbm, wg_hbm))
    ]
    for w, ref in (
        (f1_hbm, f1_ref), (f2_hbm, f2_ref), (gain1_hbm, gain1_ref), (gain2_hbm, gain2_ref), (wo_hbm, wo_ref),
        (bias_hbm, bias_ref), (pw_hbm, pw_ref),
    ):
        ins.append(pltpu.make_async_copy(w, ref, sem_in.at[len(ins)]))
    for copy in ins:
        copy.start()

    pl.semaphore_wait(barrier, (Z - 1) + (XC * H - 1) + H + jnp.where(edge, XC * H2, 0))
    loc1.wait()
    loc1c.wait()

    def a1(o):
        t = zz(o)
        return rcopy(xs.at[t], r1.at[z], sem_s1.at[t], sem_r1.at[z], dz(o), h)

    def a1c(o):
        t = zz(o)
        return rcopy(xsc.at[t], r1c.at[z], sem_s1c.at[t], sem_r1c.at[z], dz(o), h)

    @pl.when(edge)
    def _():
        every(Z, lambda o: a1c(o).start())

    every(Z, lambda o: a1(o).start())
    pl.semaphore_signal(ready, inc=1, device_id=(cross + xc, H - 1 - h), device_id_type=MESH)
    r1[z] = xs[z]
    r1c[z] = xsc[z]

    for copy in ins[:5]:
        copy.wait()
    wall[h, 4 * HW :, :] = jnp.concatenate(
        [f1_ref[...].astype(F32), jnp.zeros((2 * WR - 4 * HW - FC, CM), F32)], axis=0
    ).astype(BF)
    half = pl.ds(pl.multiple_of(core * WR, 16), WR)
    other = pl.ds(pl.multiple_of((1 - core) * WR, 16), WR)

    def aw(o):
        hh = peers[o]
        return rcopy(wall.at[h, half], wall.at[h, half], sem_sw.at[hh], sem_rw.at[h], d, hh)

    for o in range(1, H):
        aw(o).start()

    for copy in ins[5:]:
        copy.wait()

    def wait_r1(o):
        t = zz(o)
        rcopy(xs.at[t], r1.at[t], sem_s1.at[t], sem_r1.at[t], dz(o), h).wait_recv()

    def wait_r1c(o):
        t = zz(o)
        rcopy(xsc.at[t], r1c.at[t], sem_s1c.at[t], sem_r1c.at[t], dz(o), h).wait_recv()

    def a2c(i, t):
        return rcopy(
            s2c.at[i, t], r2.at[yh, xc], sem_s2c.at[i * XC + t], sem_r2.at[yh * XC + xc], cross + t, lo + i
        )

    @pl.when(edge)
    def _():
        each(Z, wait_r1c)
        for i in range(H2):

            def store(k, lanes, v):
                s2c[i, k, :, lanes] = v

            swap(r1c.at[:, i], tmp, store, Z, XC)
            every(XC, lambda t: a2c(i, t).start(), 0)

    each(Z, wait_r1)

    def store_s2(k, lanes, v):
        s2[k, :, lanes] = v

    swap(r1, tmp, store_s2, Z, XC)

    def a2(o):
        t = tx(o)
        return rcopy(s2.at[t], r2.at[yh, xc], sem_s2.at[t], sem_r2.at[yh * XC + xc], block + t, h)

    every(XC, lambda o: a2(o).start())
    r2[yh, xc] = s2[xc]

    row = lax.broadcasted_iota(jnp.int32, (N, 1), 0)
    src = row // (2 * G)
    mirror = (row // G) % 2
    src_h = jnp.where(mirror == 1, H - 1 - src % H, src % H)
    src_y = jnp.where(mirror == 1, oy, yh)
    at = ((row % Z) * 2 + src_y) * (H * XC) + src_h * XC + (src // H) * 2 + (row // Z) % 2
    place[...] = jnp.where(lax.broadcasted_iota(jnp.int32, (N, N), 1) == at, 1.0, 0.0).astype(BF)

    def wait_r2(o):
        t = tx(o)
        rcopy(s2.at[t], r2.at[yh, t], sem_s2.at[t], sem_r2.at[yh * XC + t], block + t, h).wait_recv()

    def wait_r2c(t):
        rcopy(s2.at[t], r2.at[oy, t], sem_s2.at[t], sem_r2.at[oy * XC + t], cross + t, h_src).wait_recv()

    each(XC, wait_r2)
    each(XC, wait_r2c, 0)

    def av(o):
        hh = peers[o]
        return rcopy(wall.at[hh, half], wall.at[hh, half], sem_sv.at[hh], sem_rv.at[hh], sib, h)

    def pass_w(o):
        hh = peers[o]
        rcopy(wall.at[hh, half], wall.at[hh, half], sem_sw.at[hh], sem_rw.at[hh], d, hh).wait_recv()
        av(o).start()

    pass_w(1)
    activity = r2[...].astype(F32).reshape(S, CM)
    normed = standardize(activity, gain1_ref[...])

    for o in range(H):
        hh = peers[o]
        if 0 < o < H - 1:
            pass_w(o + 1)
        if o > 0:
            rcopy(wall.at[hh, other], wall.at[hh, other], sem_sv.at[hh], sem_rv.at[hh], sib, h).wait_recv()
        proj = dot(wall[hh, : 4 * HW, :], normed, 1, 1)
        query = proj[:HW].astype(BF)
        keys = proj[HW : 2 * HW].astype(BF)
        values = proj[2 * HW : 3 * HW].astype(BF)
        gate = jax.nn.sigmoid(proj[3 * HW :]).astype(BF).astype(F32)
        parts = []
        for e in range(NH):
            rows = slice(e * HEAD_DIMENSION, (e + 1) * HEAD_DIMENSION)
            scores = dot(keys[rows], query[rows], 0, 0) * HEAD_DIMENSION ** (-0.5)
            weights = jnp.exp(scores - jnp.max(scores, axis=0, keepdims=True))
            probs = (weights / jnp.sum(weights, axis=0, keepdims=True)).astype(BF)
            parts.append((dot(values[rows], probs, 1, 0) * gate[rows]).astype(BF))
        mixed[pl.ds(pl.multiple_of(hh * HW, HW), HW), :] = jnp.concatenate(parts, axis=0)
    after = (activity + dot(mixed[...], wo_ref[...], 0, 0)).astype(BF).astype(F32)
    acol[...] = after.reshape(2, XC, Z, CM).astype(BF)
    def aa1(o):
        t = tx(o)
        return rcopy(acol.at[:, t], ra1.at[xc], sem_sa1.at[t], sem_ra1.at[xc], block + t, h)

    every(XC, lambda o: aa1(o).start())
    ra1[xc] = acol[:, xc]

    normed2 = standardize(after, gain2_ref[...])
    f1 = jnp.concatenate([wall[k, 4 * HW :, :].astype(F32)[:FC] for k in range(H)], axis=0).astype(BF)
    lcol[...] = dot(f1, normed2, 1, 1).astype(BF)
    rcol[...] = dot(f2_ref[...], normed2, 1, 1).astype(BF)

    def al1(o):
        return rcopy(lcol, l1.at[z], sem_sl1.at[o], sem_rl1.at[z], dz(o), h)

    def al1m(o):
        return rcopy(lcol, l1.at[Z + z], sem_sl1.at[Z + o], sem_rl1.at[Z + z], dm(o), H - 1 - h)

    pl.semaphore_wait(ready, 1)
    every(Z, lambda o: al1m(o).start(), 0)
    every(Z, lambda o: al1(o).start())
    l1[z] = lcol[...]

    core_d = div(xc, H)
    slot = rem(xc, H)
    far = core != core_d

    def ar(o):
        hh = th(o)
        return rcopy(rcol, rights.at[h], sem_sr.at[hh], sem_rr.at[h], d, hh)

    every(H, lambda o: ar(o).start())
    rights[h] = rcol[...]

    def ax1(o):
        return rcopy(
            rights, right.at[:, slot], sem_sq.at[o], sem_rq.at[slot], block + 2 * rem(xx + o, X) + core_d, h
        )

    def pass_right():
        for o in range(1, H):
            hh = th(o)
            rcopy(rcol, rights.at[hh], sem_sr.at[hh], sem_rr.at[hh], d, hh).wait_recv()
        for o in range(1, X):
            ax1(o).start()

        @pl.when(far)
        def _():
            ax1(0).start()

        @pl.when(jnp.logical_not(far))
        def _():
            right[:, slot] = rights[...]

    def wait_a1(o):
        t = tx(o)
        rcopy(acol.at[:, t], ra1.at[t], sem_sa1.at[t], sem_ra1.at[t], block + t, h).wait_recv()

    each(XC, wait_a1)

    def store_a2(k, lanes, v):
        sa2[k // Z, k % Z, :, lanes] = v

    swap(ra1, tmpa, store_a2, XC, G)

    def aa2(o):
        t = zz(o)
        return rcopy(sa2.at[:, t], ra2.at[:, z], sem_sa2.at[t], sem_ra2.at[z], dz(o), h)

    every(Z, lambda o: aa2(o).start())
    ra2[:, z] = sa2[:, z]

    def aa3(t, o):
        return rcopy(
            ra2.at[yh, pl.ds(t, 2)], o0_ref.at[pl.ds(t, 2), yh, h], sem_sa3.at[o], sem_ra3.at[yh * H + h],
            block + xc, th(o),
        )

    def aa3c(t, o):
        return rcopy(
            ra2.at[oy, pl.ds(t, 2)], o0_ref.at[pl.ds(t, 2), yh, h], sem_sa3.at[H + o], sem_ra3.at[yh * H + h],
            cross + xc, o,
        )

    def wait_a2(t):
        rcopy(sa2.at[:, t], ra2.at[:, t], sem_sa2.at[t], sem_ra2.at[t], d, h).wait_recv()

    def ring(q):
        t = 2 * rem(div(z, 2) + q, Z // 2)
        if q == 0:
            wait_a2(t + 1 - rem(z, 2))
        else:
            wait_a2(t)
            wait_a2(t + 1)
        for o in range(H):
            aa3c(t, o).start()
        for o in range(1, H):
            aa3(t, o).start()

    pass_right()
    pairs = sorted(range(Z // 2), key=lambda q: min(q, Z // 2 - q))
    ring(0)

    def wait_l1(k):
        rcopy(lcol, l1.at[k], sem_sl1.at[0], sem_rl1.at[k], d, h).wait_recv()

    def al3(side):
        part = left.at[side, :, core]
        return rcopy(part, part, sem_sl3.at[side], sem_rl3.at[side], sib, h)

    def wait_l3(side):
        part = left.at[side, :, 1 - core]
        rcopy(part, part, sem_sl3.at[side], sem_rl3.at[side], sib, h).wait_recv()

    def left_side(side):
        tmpl[...] = l1[side * Z : (side + 1) * Z].astype(F32).reshape(Z * CC, S)
        for c in range(CC):
            left[side, c, core] = tmpl[pl.ds(c, Z, stride=CC), :].astype(BF)
        al3(side).start()

    each(Z, lambda o: wait_l1(zz(o)))
    left_side(0)

    for k in range(H):
        from_xc = core * H + k

        @pl.when(from_xc != xc)
        def _():
            rcopy(rights, right.at[:, k], sem_sq.at[0], sem_rq.at[k], block + from_xc, h).wait_recv()

    own = xx * H + h

    def ax(side, x2, hh):
        k = (side * X + x2) * H + hh
        return rcopy(
            res.at[side, x2 * H + hh], rx.at[own, side], sem_sx.at[k], sem_rx.at[own * 2 + side],
            block + 2 * x2 + core, hh,
        )

    def pair_half(side):
        lefts = left[side].astype(F32).reshape(CC * G, S).astype(BF)
        flats = []
        for x2 in range(X):
            outer = dot(lefts, right[x2].reshape(H * CC, S), 1, 1) * (1.0 / S)
            flat = [[] for _ in range(H)]
            for c in range(0, CC, H):
                for k, part in enumerate(turn([outer[(c + r) * G : (c + r + 1) * G] for r in range(H)])):
                    flat[k].append(part.astype(BF))
            flats += [jnp.concatenate(f, axis=1) for f in flat]
        total = jnp.dot(jnp.concatenate(flats, axis=0), pw_ref[...], preferred_element_type=F32) + bias_ref[...]
        for x2 in range(X):
            base = x2 * H * G
            for hh, part in enumerate(turn([total[base + k * G : base + (k + 1) * G] for k in range(H)])):
                res[side, x2 * H + hh] = part.astype(BF)
                here = (x2 == xx) & (hh == h)

                @pl.when(here)
                def _():
                    rx[own, side] = res[side, x2 * H + hh]

                @pl.when(jnp.logical_not(here))
                def _():
                    ax(side, x2, hh).start()

    for q in pairs[1:3]:
        ring(q)
    wait_l3(0)
    pair_half(0)
    for q in pairs[3:]:
        ring(q)

    each(Z, lambda o: wait_l1(Z + o), 0)
    left_side(1)
    o0_ref[:, yh, h] = ra2[yh]
    wait_l3(1)
    pair_half(1)

    for x2 in range(X):
        for hh in range(H):
            k = x2 * H + hh

            @pl.when(k != own)
            def _():
                for c in range(2):
                    rcopy(
                        res.at[0, k], rx.at[k, c], sem_sx.at[k], sem_rx.at[k * 2 + c], block + 2 * x2 + core, hh
                    ).wait_recv()

    o1_ref[...] = dot(rx[...].reshape(N, CZ), place[...], 0, 0).astype(BF)

    def wait_a3(o):
        hh = th(o)
        rcopy(ra2.at[yh], o0_ref.at[:, yh, hh], sem_sa3.at[o], sem_ra3.at[yh * H + hh], d, hh).wait()

    def wait_a3c(o):
        rcopy(ra2.at[oy], o0_ref.at[:, oy, o], sem_sa3.at[H + o], sem_ra3.at[oy * H + o], cross + xc, o).wait()

    each(H, wait_a3)
    each(H, wait_a3c, 0)
    each(Z, lambda o: a1(o).wait_send())

    @pl.when(edge)
    def _():
        each(Z, lambda o: a1c(o).wait_send())
        for i in range(H2):
            each(XC, lambda t: a2c(i, t).wait_send(), 0)

    for o in range(1, H):
        aw(o).wait_send()
        av(o).wait_send()
    each(XC, lambda o: a2(o).wait_send())
    each(Z, lambda o: al1m(o).wait_send(), 0)
    each(Z, lambda o: al1(o).wait_send())

    each(H, lambda o: ar(o).wait_send())
    for o in range(1, X):
        ax1(o).wait_send()

    @pl.when(far)
    def _():
        ax1(0).wait_send()

    each(XC, lambda o: aa1(o).wait_send())
    each(Z, lambda o: aa2(o).wait_send())
    al3(0).wait_send()
    al3(1).wait_send()
    for side in range(2):
        for x2 in range(X):
            for hh in range(H):

                @pl.when(x2 * H + hh != own)
                def _():
                    ax(side, x2, hh).wait_send()


def shards(mesh, x, gain1, wq, wk, wv, wg, wo, gain2, f1, f2, pw, bias):
    D, H = mesh.shape["dap"], mesh.shape["head"]
    G, X = D // XC, XC // 2
    Z = G // 2
    S = D
    CM = x.shape[2]
    HW, FC, CC, CZ = wq.shape[1], f1.shape[1], f2.shape[1], pw.shape[1]
    vm = pl.BlockSpec(memory_space=pltpu.VMEM)
    hbm = pl.BlockSpec(memory_space=pltpu.HBM)
    dma = pltpu.SemaphoreType.DMA
    scratch = [
        pltpu.VMEM((H, 4 * HW + 32, CM), BF),
        pltpu.VMEM((CM, CM), BF),
        pltpu.VMEM((1, CM), F32),
        pltpu.VMEM((1, CM), F32),
        pltpu.VMEM((FC, CM), BF),
        pltpu.VMEM((CC, CM), BF),
        pltpu.VMEM((CC * CC, CZ), BF),
        pltpu.VMEM((1, CZ), F32),
        pltpu.VMEM((S * H, S * H), BF),
        pltpu.VMEM((Z, XC, CM), BF),
        pltpu.VMEM((Z, H // 2, XC, CM), BF),
        pltpu.VMEM((Z, XC, CM), BF),
        pltpu.VMEM((Z, H // 2, XC, CM), BF),
        pltpu.VMEM((CM // 128, Z * XC, 128), F32),
        pltpu.VMEM((XC, Z, CM), BF),
        pltpu.VMEM((H // 2, XC, Z, CM), BF),
        pltpu.VMEM((2, XC, Z, CM), BF),
        pltpu.VMEM((CM, S), BF),
        pltpu.VMEM((2, XC, Z, CM), BF),
        pltpu.VMEM((CC, S), BF),
        pltpu.VMEM((CC, S), BF),
        pltpu.VMEM((G, CC, S), BF),
        pltpu.VMEM((Z * CC, S), F32),
        pltpu.VMEM((2, CC, 2, Z, S), BF),
        pltpu.VMEM((H, CC, S), BF),
        pltpu.VMEM((X, H, CC, S), BF),
        pltpu.VMEM((2, X * H, G, CZ), BF),
        pltpu.VMEM((X * H, 2, G, CZ), BF),
        pltpu.VMEM((XC, 2, Z, CM), BF),
        pltpu.VMEM((CM // 128, S, 128), F32),
        pltpu.VMEM((2, Z, XC, CM), BF),
        pltpu.VMEM((2, Z, XC, CM), BF),
    ]
    sems = [
        Z, Z, Z, Z, H, H, H, H, XC, H // 2 * XC, 2 * XC, G, G,
        2, 2, H, H, X, H, XC, XC, Z, Z, 2 * H, 2 * H, 2 * X * H, 2 * X * H,
        2, 11,
    ]
    scratch += [dma if n is None else dma((n,)) for n in sems]
    scratch.append(pltpu.SemaphoreType.REGULAR)
    o0, o1 = pl.pallas_call(
        functools.partial(kernel, (Z, H, CM)),
        out_shape=(
            pltpu.VMEM((Z, 2, H, XC, CM), BF),
            pltpu.VMEM((CZ, H * S), BF),
        ),
        in_specs=[hbm] * 12,
        out_specs=(vm, vm),
        scratch_shapes=scratch,
        compiler_params=pltpu.CompilerParams(
            collective_id=0, has_side_effects=True, vmem_limit_bytes=60 * 1024 * 1024
        ),
    )(
        x.reshape(Z, 2, H, XC, CM), wq.T, wk.T, wv.T, wg.T, wo, gain1.reshape(1, CM), gain2.reshape(1, CM), f1.T, f2.T,
        pw, bias.reshape(1, CZ),
    )
    return o0.reshape(1, H * S, CM), o1.reshape(H, CZ // H, H * S).transpose(2, 0, 1)


def solution(mesh):
    placed = (
        P("dap", None, None),
        P(),
        P(None, "head"),
        P(None, "head"),
        P(None, "head"),
        P(None, "head"),
        P(),
        P(),
        P(None, "head"),
        P(),
        P(),
        P(),
    )
    return jax.shard_map(
        functools.partial(shards, mesh),
        mesh=mesh,
        in_specs=placed,
        out_specs=(P("dap", None, None), P(None, "dap", "head")),
        check_vma=False,
    )
```

```python
import functools

import jax
import jax.numpy as jnp
from jax import lax
from jax.experimental import pallas as pl
from jax.experimental.pallas import tpu as pltpu
from jax.sharding import PartitionSpec as P

MESH = pl.DeviceIdType.MESH
HEAD_DIMENSION = 32
XC = 8
EPS = 1e-05
BF = jnp.bfloat16
F32 = jnp.float32


def dot(a, b, ca, cb):
    return lax.dot_general(a, b, (((ca,), (cb,)), ((), ())), preferred_element_type=F32)


def standardize(v, gain):
    mean = jnp.mean(v, axis=-1, keepdims=True)
    centred = v - mean
    variance = jnp.mean(centred * centred, axis=-1, keepdims=True)
    return (centred * lax.rsqrt(variance + EPS) * gain).astype(BF)


def rem(a, n):
    return lax.rem(a, jnp.int32(n))


def div(a, n):
    return lax.div(a, jnp.int32(n))


def swap(src, tmp, store, a, b):
    for i in range(src.shape[-1] // 128):
        lanes = slice(i * 128, (i + 1) * 128)
        tmp[i] = src[..., lanes].astype(F32).reshape(a * b, 128)
        for k in range(b):
            store(k, lanes, tmp[i, pl.ds(k, a, stride=b), :].astype(BF))


def turn(mats):
    n = len(mats)
    width = mats[0].shape[1]
    lane = lax.broadcasted_iota(jnp.int32, (1, width), 1)
    mats = list(mats)
    dist = n // 2
    while dist >= 1:
        lanes = dist * (width // n)
        low = (lane // lanes) % 2 == 0
        out = list(mats)
        for r in range(n):
            if (r // dist) % 2 == 0:
                a, b = mats[r], mats[r + dist]
                out[r] = jnp.where(low, a, pltpu.roll(b, lanes, 1))
                out[r + dist] = jnp.where(low, pltpu.roll(a, width - lanes, 1), b)
        mats = out
        dist //= 2
    return mats


def kernel(
    dims,
    x_hbm, wq_hbm, wk_hbm, wv_hbm, wg_hbm, wo_hbm, gain1_hbm, gain2_hbm, f1_hbm, f2_hbm, pw_hbm, bias_hbm,
    o0_ref, o1_ref,
    wall, wo_ref, gain1_ref, gain2_ref, f1_ref, f2_ref, pw_ref, bias_ref, place,
    xs, xsc, r1, r1c, tmp, s2, s2c, r2, mixed, acol, lcol, rcol, l1, tmpl, left, rights, right, res, rx, ra1, tmpa, sa2, ra2,
    sem_s1, sem_r1, sem_s1c, sem_r1c, sem_sw, sem_rw, sem_sv, sem_rv, sem_s2, sem_s2c, sem_r2, sem_sl1, sem_rl1,
    sem_sl3, sem_rl3, sem_sr, sem_rr, sem_sq, sem_rq, sem_sa1, sem_ra1, sem_sa2, sem_ra2, sem_sa3, sem_ra3, sem_sx, sem_rx,
    sem_loc, sem_in, ready,
):
    Z, H, CM = dims
    X = XC // 2
    H2 = H // 2
    G = 2 * Z
    S = G * XC
    N = S * H
    HW = wq_hbm.shape[0]
    NH = HW // HEAD_DIMENSION
    FC = f1_hbm.shape[0]
    CC = f2_hbm.shape[0]
    CZ = pw_hbm.shape[1]
    WR = wall.shape[1] // 2
    d = lax.axis_index("dap")
    h = lax.axis_index("head")
    z = div(d, 2 * XC)
    yh = rem(div(d, XC), 2)
    xc = rem(d, XC)
    xx = div(xc, 2)
    core = rem(xc, 2)
    oy = 1 - yh
    block = (z * 2 + yh) * XC
    cross = (z * 2 + oy) * XC
    sib = block + 2 * xx + (1 - core)
    edge = (h == 0) | (h == H - 1)
    lo = jnp.where(h == 0, H2, 0)
    h_src = jnp.where(h < H2, H - 1, 0)

    def rcopy(src, dst, ssem, rsem, dd, hh):
        return pltpu.make_async_remote_copy(
            src_ref=src, dst_ref=dst, send_sem=ssem, recv_sem=rsem, device_id=(dd, hh), device_id_type=MESH
        )

    def each(n, f, first=1):
        def step(o, c):
            f(o)
            return c

        if n > first:
            lax.fori_loop(first, n, step, 0)

    def every(n, f, first=1):
        for o in range(first, n):
            f(o)

    distant = sorted(range(Z), key=lambda o: -min(o, Z - o))

    def zz(o):
        return rem(z + o, Z)

    def dz(o):
        return (zz(o) * 2 + yh) * XC + xc

    def dm(o):
        return (zz(o) * 2 + oy) * XC + xc

    def tx(o):
        return rem(xc + o, XC)

    def th(o):
        return rem(h + o, H)

    peers = [h, h + 1 - 2 * rem(h, 2), rem(h + 2, 4), 3 - h] if H == 4 else [th(o) for o in range(H)]

    barrier = pltpu.get_barrier_semaphore()

    def signal(dd, hh):
        pl.semaphore_signal(barrier, inc=1, device_id=(dd, hh), device_id_type=MESH)

    for o in sorted(range(1, Z), key=lambda o: -min(o, Z - o)):
        signal(dz(o), h)
    loc1 = pltpu.make_async_copy(x_hbm.at[:, yh, h], xs, sem_loc.at[0])
    loc1c = pltpu.make_async_copy(x_hbm.at[:, oy, pl.ds(lo, H2)], xsc, sem_loc.at[1])
    loc1.start()
    loc1c.start()
    for o in range(1, XC):
        signal(block + tx(o), h)
    for o in range(XC):
        signal(cross + o, h_src)
    for o in range(H):
        signal(cross + xc, o)
    for k in range(1, H):
        hh = th(k)
        for o in range(XC):
            signal(block + o, hh)

    ins = [
        pltpu.make_async_copy(w, wall.at[h, pl.ds(i * HW, HW)], sem_in.at[i])
        for i, w in enumerate((wq_hbm, wk_hbm, wv_hbm, wg_hbm))
    ]
    for w, ref in (
        (f1_hbm, f1_ref), (f2_hbm, f2_ref), (gain1_hbm, gain1_ref), (gain2_hbm, gain2_ref), (wo_hbm, wo_ref),
        (bias_hbm, bias_ref), (pw_hbm, pw_ref),
    ):
        ins.append(pltpu.make_async_copy(w, ref, sem_in.at[len(ins)]))
    for copy in ins:
        copy.start()

    pl.semaphore_wait(barrier, (Z - 1) + (XC * H - 1) + H + jnp.where(edge, XC * H2, 0))
    loc1.wait()
    loc1c.wait()

    def a1(o):
        t = zz(o)
        return rcopy(xs.at[t], r1.at[z], sem_s1.at[t], sem_r1.at[z], dz(o), h)

    def a1c(o):
        t = zz(o)
        return rcopy(xsc.at[t], r1c.at[z], sem_s1c.at[t], sem_r1c.at[z], dz(o), h)

    @pl.when(edge)
    def _():
        for o in distant[:-1]:
            a1c(o).start()

    for o in distant[:-1]:
        a1(o).start()
    pl.semaphore_signal(ready, inc=1, device_id=(cross + xc, H - 1 - h), device_id_type=MESH)
    r1[z] = xs[z]
    r1c[z] = xsc[z]

    for copy in ins[:5]:
        copy.wait()
    wall[h, 4 * HW :, :] = jnp.concatenate(
        [f1_ref[...].astype(F32), jnp.zeros((2 * WR - 4 * HW - FC, CM), F32)], axis=0
    ).astype(BF)
    half = pl.ds(pl.multiple_of(core * WR, 16), WR)
    other = pl.ds(pl.multiple_of((1 - core) * WR, 16), WR)

    def aw(o):
        hh = peers[o]
        return rcopy(wall.at[h, half], wall.at[h, half], sem_sw.at[hh], sem_rw.at[h], d, hh)

    for o in range(1, H):
        aw(o).start()

    for copy in ins[5:]:
        copy.wait()

    def wait_r1(o):
        t = zz(o)
        rcopy(xs.at[t], r1.at[t], sem_s1.at[t], sem_r1.at[t], dz(o), h).wait_recv()

    def wait_r1c(o):
        t = zz(o)
        rcopy(xsc.at[t], r1c.at[t], sem_s1c.at[t], sem_r1c.at[t], dz(o), h).wait_recv()

    def a2c(i, t):
        return rcopy(
            s2c.at[i, t], r2.at[yh, xc], sem_s2c.at[i * XC + t], sem_r2.at[yh * XC + xc], cross + t, lo + i
        )

    @pl.when(edge)
    def _():
        each(Z, wait_r1c)
        for i in range(H2):

            def store(k, lanes, v):
                s2c[i, k, :, lanes] = v

            swap(r1c.at[:, i], tmp, store, Z, XC)
            every(XC, lambda t: a2c(i, t).start(), 0)

    each(Z, wait_r1)

    def store_s2(k, lanes, v):
        s2[k, :, lanes] = v

    swap(r1, tmp, store_s2, Z, XC)

    def a2(o):
        t = tx(o)
        return rcopy(s2.at[t], r2.at[yh, xc], sem_s2.at[t], sem_r2.at[yh * XC + xc], block + t, h)

    every(XC, lambda o: a2(o).start())
    r2[yh, xc] = s2[xc]

    row = lax.broadcasted_iota(jnp.int32, (N, 1), 0)
    src = row // (2 * G)
    mirror = (row // G) % 2
    src_h = jnp.where(mirror == 1, H - 1 - src % H, src % H)
    src_y = jnp.where(mirror == 1, oy, yh)
    at = ((row % Z) * 2 + src_y) * (H * XC) + src_h * XC + (src // H) * 2 + (row // Z) % 2
    place[...] = jnp.where(lax.broadcasted_iota(jnp.int32, (N, N), 1) == at, 1.0, 0.0).astype(BF)

    def wait_r2(o):
        t = tx(o)
        rcopy(s2.at[t], r2.at[yh, t], sem_s2.at[t], sem_r2.at[yh * XC + t], block + t, h).wait_recv()

    def wait_r2c(t):
        rcopy(s2.at[t], r2.at[oy, t], sem_s2.at[t], sem_r2.at[oy * XC + t], cross + t, h_src).wait_recv()

    each(XC, wait_r2)
    each(XC, wait_r2c, 0)

    def av(o):
        hh = peers[o]
        return rcopy(wall.at[hh, half], wall.at[hh, half], sem_sv.at[hh], sem_rv.at[hh], sib, h)

    def pass_w(o):
        hh = peers[o]
        rcopy(wall.at[hh, half], wall.at[hh, half], sem_sw.at[hh], sem_rw.at[hh], d, hh).wait_recv()
        av(o).start()

    pass_w(1)
    activity = r2[...].astype(F32).reshape(S, CM)
    normed = standardize(activity, gain1_ref[...])

    for o in range(H):
        hh = peers[o]
        if 0 < o < H - 1:
            pass_w(o + 1)
        if o > 0:
            rcopy(wall.at[hh, other], wall.at[hh, other], sem_sv.at[hh], sem_rv.at[hh], sib, h).wait_recv()
        proj = dot(wall[hh, : 4 * HW, :], normed, 1, 1)
        query = proj[:HW].astype(BF)
        keys = proj[HW : 2 * HW].astype(BF)
        values = proj[2 * HW : 3 * HW].astype(BF)
        gate = jax.nn.sigmoid(proj[3 * HW :]).astype(BF).astype(F32)
        parts = []
        for e in range(NH):
            rows = slice(e * HEAD_DIMENSION, (e + 1) * HEAD_DIMENSION)
            scores = dot(keys[rows], query[rows], 0, 0) * HEAD_DIMENSION ** (-0.5)
            weights = jnp.exp(scores - jnp.max(scores, axis=0, keepdims=True))
            probs = (weights / jnp.sum(weights, axis=0, keepdims=True)).astype(BF)
            parts.append((dot(values[rows], probs, 1, 0) * gate[rows]).astype(BF))
        mixed[pl.ds(pl.multiple_of(hh * HW, HW), HW), :] = jnp.concatenate(parts, axis=0)
    after = (activity + dot(mixed[...], wo_ref[...], 0, 0)).astype(BF).astype(F32)
    acol[...] = after.reshape(2, XC, Z, CM).astype(BF)
    def aa1(o):
        t = tx(o)
        return rcopy(acol.at[:, t], ra1.at[xc], sem_sa1.at[t], sem_ra1.at[xc], block + t, h)

    every(XC, lambda o: aa1(o).start())
    ra1[xc] = acol[:, xc]

    normed2 = standardize(after, gain2_ref[...])
    f1 = jnp.concatenate([wall[k, 4 * HW :, :].astype(F32)[:FC] for k in range(H)], axis=0).astype(BF)
    lcol[...] = dot(f1, normed2, 1, 1).astype(BF)
    rcol[...] = dot(f2_ref[...], normed2, 1, 1).astype(BF)

    def al1(o):
        return rcopy(lcol, l1.at[z], sem_sl1.at[o], sem_rl1.at[z], dz(o), h)

    def al1m(o):
        return rcopy(lcol, l1.at[Z + z], sem_sl1.at[Z + o], sem_rl1.at[Z + z], dm(o), H - 1 - h)

    pl.semaphore_wait(ready, 1)
    for o in distant:
        al1m(o).start()
    for o in distant[:-1]:
        al1(o).start()
    l1[z] = lcol[...]

    core_d = div(xc, H)
    slot = rem(xc, H)
    far = core != core_d

    def ar(o):
        hh = th(o)
        return rcopy(rcol, rights.at[h], sem_sr.at[hh], sem_rr.at[h], d, hh)

    every(H, lambda o: ar(o).start())
    rights[h] = rcol[...]

    def ax1(o):
        return rcopy(
            rights, right.at[:, slot], sem_sq.at[o], sem_rq.at[slot], block + 2 * rem(xx + o, X) + core_d, h
        )

    def pass_right():
        for o in range(1, H):
            hh = th(o)
            rcopy(rcol, rights.at[hh], sem_sr.at[hh], sem_rr.at[hh], d, hh).wait_recv()
        for o in range(1, X):
            ax1(o).start()

        @pl.when(far)
        def _():
            ax1(0).start()

        @pl.when(jnp.logical_not(far))
        def _():
            right[:, slot] = rights[...]

    def wait_a1(o):
        t = tx(o)
        rcopy(acol.at[:, t], ra1.at[t], sem_sa1.at[t], sem_ra1.at[t], block + t, h).wait_recv()

    each(XC, wait_a1)

    def store_a2(k, lanes, v):
        sa2[k // Z, k % Z, :, lanes] = v

    swap(ra1, tmpa, store_a2, XC, G)

    def aa2(o):
        t = zz(o)
        return rcopy(sa2.at[:, t], ra2.at[:, z], sem_sa2.at[t], sem_ra2.at[z], dz(o), h)

    for o in distant[:-1]:
        aa2(o).start()
    ra2[:, z] = sa2[:, z]

    def aa3(t, o):
        return rcopy(
            ra2.at[yh, pl.ds(t, 2)], o0_ref.at[pl.ds(t, 2), yh, h], sem_sa3.at[o], sem_ra3.at[yh * H + h],
            block + xc, th(o),
        )

    def aa3c(t, o):
        return rcopy(
            ra2.at[oy, pl.ds(t, 2)], o0_ref.at[pl.ds(t, 2), yh, h], sem_sa3.at[H + o], sem_ra3.at[yh * H + h],
            cross + xc, o,
        )

    def wait_a2(t):
        rcopy(sa2.at[:, t], ra2.at[:, t], sem_sa2.at[t], sem_ra2.at[t], d, h).wait_recv()

    def ring(q):
        t = 2 * rem(div(z, 2) + q, Z // 2)
        if q == 0:
            wait_a2(t + 1 - rem(z, 2))
        else:
            wait_a2(t)
            wait_a2(t + 1)
        for o in range(H):
            aa3c(t, o).start()
        for o in range(1, H):
            aa3(t, o).start()

    pass_right()
    pairs = sorted(range(Z // 2), key=lambda q: min(q, Z // 2 - q))
    ring(0)

    def wait_l1(k):
        rcopy(lcol, l1.at[k], sem_sl1.at[0], sem_rl1.at[k], d, h).wait_recv()

    def al3(side):
        part = left.at[side, :, core]
        return rcopy(part, part, sem_sl3.at[side], sem_rl3.at[side], sib, h)

    def wait_l3(side):
        part = left.at[side, :, 1 - core]
        rcopy(part, part, sem_sl3.at[side], sem_rl3.at[side], sib, h).wait_recv()

    def left_side(side):
        tmpl[...] = l1[side * Z : (side + 1) * Z].astype(F32).reshape(Z * CC, S)
        for c in range(CC):
            left[side, c, core] = tmpl[pl.ds(c, Z, stride=CC), :].astype(BF)
        al3(side).start()

    each(Z, lambda o: wait_l1(zz(o)))
    left_side(0)

    for k in range(H):
        from_xc = core * H + k

        @pl.when(from_xc != xc)
        def _():
            rcopy(rights, right.at[:, k], sem_sq.at[0], sem_rq.at[k], block + from_xc, h).wait_recv()

    own = xx * H + h

    def ax(side, x2, hh):
        k = (side * X + x2) * H + hh
        return rcopy(
            res.at[side, x2 * H + hh], rx.at[own, side], sem_sx.at[k], sem_rx.at[own * 2 + side],
            block + 2 * x2 + core, hh,
        )

    def pair_half(side):
        lefts = left[side].astype(F32).reshape(CC * G, S).astype(BF)
        flats = []
        for x2 in range(X):
            outer = dot(lefts, right[x2].reshape(H * CC, S), 1, 1) * (1.0 / S)
            flat = [[] for _ in range(H)]
            for c in range(0, CC, H):
                for k, part in enumerate(turn([outer[(c + r) * G : (c + r + 1) * G] for r in range(H)])):
                    flat[k].append(part.astype(BF))
            flats += [jnp.concatenate(f, axis=1) for f in flat]
        total = jnp.dot(jnp.concatenate(flats, axis=0), pw_ref[...], preferred_element_type=F32) + bias_ref[...]
        for x2 in range(X):
            base = x2 * H * G
            for hh, part in enumerate(turn([total[base + k * G : base + (k + 1) * G] for k in range(H)])):
                res[side, x2 * H + hh] = part.astype(BF)
                here = (x2 == xx) & (hh == h)

                @pl.when(here)
                def _():
                    rx[own, side] = res[side, x2 * H + hh]

                @pl.when(jnp.logical_not(here))
                def _():
                    ax(side, x2, hh).start()

    for q in pairs[1:3]:
        ring(q)
    wait_l3(0)
    pair_half(0)
    for q in pairs[3:]:
        ring(q)

    each(Z, lambda o: wait_l1(Z + o), 0)
    left_side(1)
    o0_ref[:, yh, h] = ra2[yh]
    wait_l3(1)
    pair_half(1)

    for x2 in range(X):
        for hh in range(H):
            k = x2 * H + hh

            @pl.when(k != own)
            def _():
                for c in range(2):
                    rcopy(
                        res.at[0, k], rx.at[k, c], sem_sx.at[k], sem_rx.at[k * 2 + c], block + 2 * x2 + core, hh
                    ).wait_recv()

    o1_ref[...] = dot(rx[...].reshape(N, CZ), place[...], 0, 0).astype(BF)

    def wait_a3(o):
        hh = th(o)
        rcopy(ra2.at[yh], o0_ref.at[:, yh, hh], sem_sa3.at[o], sem_ra3.at[yh * H + hh], d, hh).wait()

    def wait_a3c(o):
        rcopy(ra2.at[oy], o0_ref.at[:, oy, o], sem_sa3.at[H + o], sem_ra3.at[oy * H + o], cross + xc, o).wait()

    each(H, wait_a3)
    each(H, wait_a3c, 0)
    each(Z, lambda o: a1(o).wait_send())

    @pl.when(edge)
    def _():
        each(Z, lambda o: a1c(o).wait_send())
        for i in range(H2):
            each(XC, lambda t: a2c(i, t).wait_send(), 0)

    for o in range(1, H):
        aw(o).wait_send()
        av(o).wait_send()
    each(XC, lambda o: a2(o).wait_send())
    each(Z, lambda o: al1m(o).wait_send(), 0)
    each(Z, lambda o: al1(o).wait_send())

    each(H, lambda o: ar(o).wait_send())
    for o in range(1, X):
        ax1(o).wait_send()

    @pl.when(far)
    def _():
        ax1(0).wait_send()

    each(XC, lambda o: aa1(o).wait_send())
    each(Z, lambda o: aa2(o).wait_send())
    al3(0).wait_send()
    al3(1).wait_send()
    for side in range(2):
        for x2 in range(X):
            for hh in range(H):

                @pl.when(x2 * H + hh != own)
                def _():
                    ax(side, x2, hh).wait_send()


def shards(mesh, x, gain1, wq, wk, wv, wg, wo, gain2, f1, f2, pw, bias):
    D, H = mesh.shape["dap"], mesh.shape["head"]
    G, X = D // XC, XC // 2
    Z = G // 2
    S = D
    CM = x.shape[2]
    HW, FC, CC, CZ = wq.shape[1], f1.shape[1], f2.shape[1], pw.shape[1]
    vm = pl.BlockSpec(memory_space=pltpu.VMEM)
    hbm = pl.BlockSpec(memory_space=pltpu.HBM)
    dma = pltpu.SemaphoreType.DMA
    scratch = [
        pltpu.VMEM((H, 4 * HW + 32, CM), BF),
        pltpu.VMEM((CM, CM), BF),
        pltpu.VMEM((1, CM), F32),
        pltpu.VMEM((1, CM), F32),
        pltpu.VMEM((FC, CM), BF),
        pltpu.VMEM((CC, CM), BF),
        pltpu.VMEM((CC * CC, CZ), BF),
        pltpu.VMEM((1, CZ), F32),
        pltpu.VMEM((S * H, S * H), BF),
        pltpu.VMEM((Z, XC, CM), BF),
        pltpu.VMEM((Z, H // 2, XC, CM), BF),
        pltpu.VMEM((Z, XC, CM), BF),
        pltpu.VMEM((Z, H // 2, XC, CM), BF),
        pltpu.VMEM((CM // 128, Z * XC, 128), F32),
        pltpu.VMEM((XC, Z, CM), BF),
        pltpu.VMEM((H // 2, XC, Z, CM), BF),
        pltpu.VMEM((2, XC, Z, CM), BF),
        pltpu.VMEM((CM, S), BF),
        pltpu.VMEM((2, XC, Z, CM), BF),
        pltpu.VMEM((CC, S), BF),
        pltpu.VMEM((CC, S), BF),
        pltpu.VMEM((G, CC, S), BF),
        pltpu.VMEM((Z * CC, S), F32),
        pltpu.VMEM((2, CC, 2, Z, S), BF),
        pltpu.VMEM((H, CC, S), BF),
        pltpu.VMEM((X, H, CC, S), BF),
        pltpu.VMEM((2, X * H, G, CZ), BF),
        pltpu.VMEM((X * H, 2, G, CZ), BF),
        pltpu.VMEM((XC, 2, Z, CM), BF),
        pltpu.VMEM((CM // 128, S, 128), F32),
        pltpu.VMEM((2, Z, XC, CM), BF),
        pltpu.VMEM((2, Z, XC, CM), BF),
    ]
    sems = [
        Z, Z, Z, Z, H, H, H, H, XC, H // 2 * XC, 2 * XC, G, G,
        2, 2, H, H, X, H, XC, XC, Z, Z, 2 * H, 2 * H, 2 * X * H, 2 * X * H,
        2, 11,
    ]
    scratch += [dma if n is None else dma((n,)) for n in sems]
    scratch.append(pltpu.SemaphoreType.REGULAR)
    o0, o1 = pl.pallas_call(
        functools.partial(kernel, (Z, H, CM)),
        out_shape=(
            pltpu.VMEM((Z, 2, H, XC, CM), BF),
            pltpu.VMEM((CZ, H * S), BF),
        ),
        in_specs=[hbm] * 12,
        out_specs=(vm, vm),
        scratch_shapes=scratch,
        compiler_params=pltpu.CompilerParams(
            collective_id=0, has_side_effects=True, vmem_limit_bytes=60 * 1024 * 1024
        ),
    )(
        x.reshape(Z, 2, H, XC, CM), wq.T, wk.T, wv.T, wg.T, wo, gain1.reshape(1, CM), gain2.reshape(1, CM), f1.T, f2.T,
        pw, bias.reshape(1, CZ),
    )
    return o0.reshape(1, H * S, CM), o1.reshape(H, CZ // H, H * S).transpose(2, 0, 1)


def solution(mesh):
    placed = (
        P("dap", None, None),
        P(),
        P(None, "head"),
        P(None, "head"),
        P(None, "head"),
        P(None, "head"),
        P(),
        P(),
        P(None, "head"),
        P(),
        P(),
        P(),
    )
    return jax.shard_map(
        functools.partial(shards, mesh),
        mesh=mesh,
        in_specs=placed,
        out_specs=(P("dap", None, None), P(None, "dap", "head")),
        check_vma=False,
    )
```
